512 devices in a mesh: dp: 4 (over z_lo), tm: 16 (over y, z_hi), patch: 8 (over x, core).
Axes of the slice: x: 4, y: 4, z: 16 (z_hi: 4, z_lo: 4; z = z_hi * 4 + z_lo), core: 2. Of those that a mesh axis runs over, the one named last changes fastest.
Arguments:
- tokens: bfloat16 [1024, 64, 1024], P(('dp', 'tm'), 'patch'), parts along dimension 0, may hold values from -6 to 6
- frame_gain: float32 [1024], replicated, may hold values from 0.5 to 4.5
- qkv_weight: bfloat16 [1024, 3072], P(None, 'tm'), may hold values from -0.1875 to 0.1875
- out_weight: bfloat16 [1024, 1024], P('tm'), may hold values from -0.1875 to 0.1875
- pool_gain: float32 [1024], replicated, may hold values from 0.5 to 4.5
- latent_gain: float32 [1024], replicated, may hold values from 0.5 to 4.5
- latents: bfloat16 [64, 1024], replicated, may hold values from -6 to 6
- query_weight: bfloat16 [1024, 1024], P(None, 'tm'), may hold values from -0.1875 to 0.1875
- kv_weight: bfloat16 [1024, 2048], P(None, 'tm'), may hold values from -0.1875 to 0.1875
- clip_starts: int32 [128], P(('dp', 'tm')), parts along dimension 0, may hold values from -7 to 248, as said below
- valid_frames: int32 [4], P('dp'), parts along dimension 0, may hold values from 128 to 256
Outputs:
- temporal_out: bfloat16 [1024, 64, 1024], P(('dp', 'tm'), 'patch'), parts along dimension 0
- pooled_latents: bfloat16 [128, 64, 1024], P(('dp', 'tm')), parts along dimension 0
The draws below stay inside these ranges and needn't reach their ends.
There are 4 independent parts, one for each index of `dp`. The reference program is written for one: setup_inputs(seed, part) draws one part's arguments, and reference() takes and returns one part's arrays. A program takes and returns all parts, laid end to end along the dimension named above; an argument that names none is the same for every part. Nothing has to cross between parts.
Inputs may be any that keep to these rules, and one draw needn't show every extreme that they name: `clip_starts`: clip c starts at frame 8 * c - k with k from 0 to 7; the first clip has k = 7 and the last k = 0.
All inputs are finite; a program needn't handle non-finite values.
Results may differ from the reference program's by a relative error of at most 0.03.
The reference program's roundings to bfloat16 on the way count: a program that leaves them out, or rounds other values in their place, can miss the bound.
Values may be sent and summed in bfloat16 or wider, within the bound.
A program may use at most 64 MiB of HBM per device.

```python
import jax
import jax.numpy as jnp
from jax import lax

D = 1024
HEADS = 16
HD = 64
LATENTS = 64
CLIP = 16
STRIDE = 8
FRAMES = 256
PATCHES = 64
CLIPS = 32


def gain_values(key, low, high):
    return jax.random.uniform(key, (D,), jnp.float32, low, high)


def draw_frame_gain(key, part):
    key = jax.random.fold_in(key, 11)
    return gain_values(key, 0.5, 1.5)


def draw_pool_gain(key, part):
    key = jax.random.fold_in(key, 23)
    return gain_values(key, 0.5, 1.5)


def draw_latent_gain(key, part):
    key = jax.random.fold_in(key, 37)
    return gain_values(key, 0.5, 1.5)


def draw_clip_starts(key, part):
    key = jax.random.fold_in(key, 41)
    back = jax.random.randint(key, (CLIPS,), 0, STRIDE, dtype=jnp.int32)
    back = back.at[0].set(STRIDE - 1).at[CLIPS - 1].set(0)
    return jnp.arange(CLIPS, dtype=jnp.int32) * STRIDE - back


def shard_levels(key, dims, pieces, least, high):
    level = 1.0
    for axis_at, blocks in pieces:
        steps = jax.random.uniform(jax.random.fold_in(jax.random.fold_in(key, 6), axis_at), (blocks,), jnp.float32, least / len(pieces), high / len(pieces))
        level = level * jnp.repeat(jnp.exp(steps), dims[axis_at] // blocks).reshape((-1,) + (1,) * (len(dims) - 1 - axis_at))
    return level


def normal_values(own_key, extent, deviation, most, shards=(), held_as=jnp.bfloat16):
    loudness = shard_levels(own_key, extent, shards, -0.22, 0.18) if shards else 1.0
    drawn = jax.random.normal(own_key, extent, jnp.float32) * deviation * loudness
    return jnp.minimum(jnp.maximum(drawn, -most), most).astype(held_as)


def setup_inputs(seed: int = 0, part: int = 0) -> dict:
    splits = jax.random.split(jax.random.key(seed), 12)
    part_keys = jax.random.split(jax.random.fold_in(splits[11], part), 12)
    tokens = normal_values(part_keys[0], (FRAMES, PATCHES, D), 1.0, 6.0, ((0, 16), (1, 8)))
    frame_gain = draw_frame_gain(jax.random.fold_in(splits[11], 71), part)
    qkv_weight = normal_values(splits[2], (D, 3 * D), D ** -0.5, 0.1875, ((1, 16),))
    out_weight = normal_values(splits[3], (D, D), D ** -0.5, 0.1875, ((0, 16),))
    pool_gain = draw_pool_gain(jax.random.fold_in(splits[11], 71), part)
    latent_gain = draw_latent_gain(jax.random.fold_in(splits[11], 71), part)
    latents = normal_values(splits[6], (LATENTS, D), 1.0, 6.0)
    query_weight = normal_values(splits[7], (D, D), D ** -0.5, 0.1875, ((1, 16),))
    kv_weight = normal_values(splits[8], (D, 2 * D), D ** -0.5, 0.1875, ((1, 16),))
    clip_starts = draw_clip_starts(jax.random.fold_in(jax.random.fold_in(splits[11], part), 71), part)
    valid_frames = jax.random.randint(part_keys[10], (1,), FRAMES // 2, FRAMES + 1).astype(jnp.int32)
    return {"tokens": tokens, "frame_gain": frame_gain, "qkv_weight": qkv_weight, "out_weight": out_weight, "pool_gain": pool_gain, "latent_gain": latent_gain, "latents": latents, "query_weight": query_weight, "kv_weight": kv_weight, "clip_starts": clip_starts, "valid_frames": valid_frames}


EPS = 1e-05
NEG = -1e+30

def layer_norm(value, gain):
    value = value.astype(jnp.float32)
    center = value - lax.optimization_barrier(jnp.mean(value, axis=-1, keepdims=True))
    spread = lax.optimization_barrier(jnp.mean(center * center, axis=-1, keepdims=True))
    return center * lax.rsqrt(spread + EPS) * gain

def rounded(value):
    return lax.optimization_barrier(value.astype(jnp.bfloat16)).astype(jnp.float32)

def reference(tokens, frame_gain, qkv_weight, out_weight, pool_gain, latent_gain, latents, query_weight, kv_weight, clip_starts, valid_frames):
    score_scale = HD ** (-0.5)
    valid = valid_frames[0]
    normed = layer_norm(tokens, frame_gain).astype(jnp.bfloat16)
    projected = jnp.dot(normed.reshape(FRAMES * PATCHES, D), qkv_weight, preferred_element_type=jnp.float32).astype(jnp.bfloat16)
    projected = projected.reshape(FRAMES, PATCHES, HEADS, 3, HD)
    key_live = (jnp.arange(FRAMES, dtype=jnp.int32) < valid)[None, None, :]

    def temporal(head):
        head_part = lax.dynamic_index_in_dim(projected, head, 2, keepdims=False).astype(jnp.float32)
        query_part = head_part[:, :, 0]
        key_part = head_part[:, :, 1]
        value_part = head_part[:, :, 2]
        scores = jnp.einsum('fpe,gpe->pfg', query_part, key_part) * score_scale
        max_score = lax.optimization_barrier(jnp.max(jnp.where(key_live, scores, -jnp.inf), axis=-1, keepdims=True))
        weights = jnp.where(key_live, jnp.exp(scores - max_score), 0.0)
        weight_total = lax.optimization_barrier(jnp.sum(weights, axis=-1))
        head_mixed = jnp.einsum('pfg,gpe->fpe', rounded(weights), value_part)
        return (head_mixed / jnp.transpose(weight_total)[:, :, None]).astype(jnp.bfloat16)
    heads_out = lax.map(temporal, jnp.arange(HEADS, dtype=jnp.int32))
    attended = jnp.transpose(heads_out, (1, 2, 0, 3)).reshape(FRAMES * PATCHES, D)
    summed = tokens.astype(jnp.float32).reshape(FRAMES * PATCHES, D) + jnp.dot(attended, out_weight, preferred_element_type=jnp.float32)
    temporal_out = summed.astype(jnp.bfloat16).reshape(FRAMES, PATCHES, D)
    pooled = layer_norm(temporal_out, pool_gain).astype(jnp.bfloat16)
    latent_normed = layer_norm(latents, latent_gain).astype(jnp.bfloat16)
    latent_queries = jnp.dot(latent_normed, query_weight, preferred_element_type=jnp.float32).astype(jnp.bfloat16)
    latent_queries = latent_queries.reshape(LATENTS, HEADS, HD).astype(jnp.float32)
    latent_kv = jnp.dot(latent_normed, kv_weight, preferred_element_type=jnp.float32).astype(jnp.bfloat16)
    latent_kv = latent_kv.reshape(LATENTS, HEADS, 2, HD).astype(jnp.float32)
    clip_kv = jnp.dot(pooled.reshape(FRAMES * PATCHES, D), kv_weight, preferred_element_type=jnp.float32).astype(jnp.bfloat16)
    clip_kv = clip_kv.reshape(FRAMES, PATCHES, HEADS, 2, HD)
    padded = jnp.pad(clip_kv, ((STRIDE, STRIDE), (0, 0), (0, 0), (0, 0), (0, 0)))
    self_scores = jnp.einsum('lhe,mhe->hlm', latent_queries, latent_kv[:, :, 0]) * score_scale

    def pool(start):
        window = lax.dynamic_slice_in_dim(padded, (start + STRIDE).astype(jnp.int32), CLIP, 0).astype(jnp.float32)
        frame_index = start + jnp.arange(CLIP, dtype=jnp.int32)
        live_mask = ((frame_index >= 0) & (frame_index < valid))[None, None, :, None]
        scores = jnp.einsum('lhe,fphe->hlfp', latent_queries, window[:, :, :, 0]) * score_scale
        max_score = jnp.maximum(lax.optimization_barrier(jnp.max(jnp.where(live_mask, scores, NEG), axis=(2, 3))), lax.optimization_barrier(jnp.max(self_scores, axis=2)))
        weights = jnp.where(live_mask, jnp.exp(scores - max_score[:, :, None, None]), 0.0)
        self_weights = jnp.exp(self_scores - max_score[:, :, None])
        weight_total = lax.optimization_barrier(jnp.sum(weights, axis=(2, 3))) + lax.optimization_barrier(jnp.sum(self_weights, axis=2))
        head_mixed = jnp.einsum('hlfp,fphe->hle', rounded(weights), window[:, :, :, 1])
        head_mixed = head_mixed + jnp.einsum('hlm,mhe->hle', rounded(self_weights), latent_kv[:, :, 1])
        result = head_mixed / weight_total[:, :, None]
        return jnp.transpose(result, (1, 0, 2)).reshape(LATENTS, D).astype(jnp.bfloat16)
    pooled_latents = lax.map(pool, clip_starts)
    return (temporal_out, pooled_latents)
```

```python
import jax
import jax.numpy as jnp
from jax import lax
from jax.experimental import pallas as pl
from jax.experimental.pallas import tpu as pltpu
from jax.sharding import PartitionSpec as P

MESH = pl.DeviceIdType.MESH
F32 = jnp.float32
BF16 = jnp.bfloat16
D = 1024
HEAD = 64
CLIP = 16
EPS = 1e-05
NEG = -1e30
SCALE = HEAD ** (-0.5)
SLOTS = 160
NEAR_FIRST = (1, 3, 2)


def layer_norm(value, gain):
    center = value - jnp.mean(value, axis=-1, keepdims=True)
    spread = jnp.mean(center * center, axis=-1, keepdims=True)
    return center * lax.rsqrt(spread + EPS) * gain


def dot(a, b):
    return jnp.dot(a, b, preferred_element_type=F32)


def dot_nt(a, b):
    return lax.dot_general(a, b, (((1,), (1,)), ((), ())), preferred_element_type=F32)


class Copies:
    def __init__(self, send_sem, recv_sem):
        self.send_sem = send_sem
        self.recv_sem = recv_sem
        self.slots = {}
        self.started = []

    def slot(self, name):
        return self.slots.setdefault(name, len(self.slots))

    def make(self, name, src, dst, device):
        slot = self.slot(name)
        return pltpu.make_async_remote_copy(
            src_ref=src,
            dst_ref=dst,
            send_sem=self.send_sem.at[slot],
            recv_sem=self.recv_sem.at[slot],
            device_id=device,
            device_id_type=MESH,
        )

    def send(self, name, src, dst, device):
        copy = self.make(name, src, dst, device)
        copy.start()
        self.started.append(copy)

    def wait(self, name, dst, device):
        self.make(name, dst, dst, device).wait_recv()

    def drain(self):
        for copy in self.started:
            copy.wait_send()


def kernel(
    starts_ref,
    valid_ref,
    tokens_ref,
    frame_gain_ref,
    qkv_ref,
    out_w_ref,
    pool_gain_ref,
    latent_gain_ref,
    latents_ref,
    query_w_ref,
    kv_w_ref,
    temporal_ref,
    pooled_ref,
    own_rows,
    rows,
    normed,
    wqkv,
    wout,
    wkv,
    att_out,
    att_in,
    summed,
    back,
    latn,
    held_queries,
    start_out,
    start_in,
    part_out,
    part_in,
    stat_out,
    stat_in,
    near_out,
    near_in,
    nstat_out,
    nstat_in,
    piece_out,
    piece_in,
    send_sem,
    recv_sem,
):
    t = lax.axis_index("tm")
    q = lax.axis_index("patch")
    y, g = t // 4, t % 4
    x, c = q // 2, q % 2
    copies = Copies(send_sem, recv_sem)

    def at_z(d):
        return (g + d) % 4

    def at_y(d):
        return (y + d) % 4

    def at_x(d):
        return ((x + d) % 4) * 2 + c

    def to_z(d):
        return {"tm": y * 4 + at_z(d)}

    def to_y(d):
        return {"tm": at_y(d) * 4 + g}

    def to_x(d):
        return {"patch": at_x(d)}

    def to_patch(d):
        return {"patch": (q + d) % 8}

    sibling = {"patch": x * 2 + 1 - c}
    after = {"tm": (t + 1) % 16}
    before = {"tm": (t + 15) % 16}

    barrier = pltpu.get_barrier_semaphore()
    partners = (
        [to_z(d) for d in (1, 2, 3)]
        + [to_y(d) for d in (1, 2, 3)]
        + [to_patch(d) for d in range(1, 8)]
        + [after, before]
    )
    for partner in partners:
        pl.semaphore_signal(barrier, inc=1, device_id=partner, device_id_type=MESH)

    to_row = lax.broadcasted_iota(jnp.int32, (128, 128), 0)
    from_row = lax.broadcasted_iota(jnp.int32, (128, 128), 1)
    by_position = jnp.where(from_row == (to_row & 15) * 8 + (to_row >> 4), 1.0, 0.0).astype(BF16)
    by_frame = jnp.where(from_row == (to_row & 7) * 16 + (to_row >> 3), 1.0, 0.0).astype(BF16)
    for half in range(2):
        cols = slice(half * 512, half * 512 + 512)
        own_rows[:, :, cols] = dot(by_position, tokens_ref[:, cols]).astype(BF16).reshape(4, 32, 512)

    value_cols = jnp.concatenate(
        [qkv_ref[0:512, 128:192].astype(F32), qkv_ref[512:1024, 128:192].astype(F32)], axis=1
    ).astype(BF16)
    wqkv[:, g] = jnp.concatenate([qkv_ref[:, 0:128], value_cols], axis=0).reshape(8, 192, 128)

    pl.semaphore_wait(barrier, len(partners))

    for d in (1, 3, 2):
        copies.send(f"rows{d}", own_rows.at[at_z(d)], rows.at[g], to_z(d))
    for d in NEAR_FIRST:
        copies.send(f"wqkv_z{d}", wqkv.at[q, g], wqkv.at[q, g], to_z(d))

    eighth = pl.ds(pl.multiple_of(q * 128, 128), 128)
    wout[q, t] = out_w_ref[:, eighth]
    for d in NEAR_FIRST:
        copies.send(f"wout_z{d}", wout.at[q, t], wout.at[q, t], to_z(d))

    latn[...] = layer_norm(latents_ref[...].astype(F32), latent_gain_ref[...]).astype(BF16)
    queries = dot(latn[...], query_w_ref[...])
    held_queries[...] = jnp.concatenate([queries, queries], axis=1).astype(BF16).reshape(4, 16, 128)
    wkv[q, t, 0:128, :] = kv_w_ref[eighth, :]
    wkv[q, t, 128:144, :] = held_queries[q // 2]
    for d in NEAR_FIRST:
        copies.send(f"wkv_z{d}", wkv.at[q, t], wkv.at[q, t], to_z(d))

    lane = lax.broadcasted_iota(jnp.int32, (8, 128), 1)
    start_out[...] = jnp.where(lane < 64, starts_ref[0], starts_ref[1])
    copies.send("start_after", start_out, start_in.at[0], after)
    copies.send("start_before", start_out, start_in.at[1], before)

    frame_gain = frame_gain_ref[...]

    def spread_rows(source):
        shard = y * 4 + source
        normed[shard] = layer_norm(rows[source].astype(F32), frame_gain).astype(BF16)
        for d in NEAR_FIRST:
            copies.send(("normed", d, spread_rows.count), normed.at[shard], normed.at[shard], to_y(d))
        spread_rows.count += 1

    spread_rows.count = 0
    rows[g] = own_rows[g]
    spread_rows(g)
    for d in NEAR_FIRST:
        copies.wait(f"rows{d}", rows.at[at_z(-d)], to_z(d))
        spread_rows(at_z(-d))

    def unit_start(name, buf, part):
        copies.send((name, "right"), part(buf, q), part(buf, q), to_x(1))
        copies.send((name, "left"), part(buf, q), part(buf, q), to_x(-1))
        copies.send((name, "core", 0), part(buf, q), part(buf, q), sibling)

    def unit_relay(name, buf, part, low, high):
        copies.wait((name, "right"), part(buf, at_x(-1)), to_x(1))
        copies.send((name, "relay_right"), low(buf, at_x(-1)), low(buf, at_x(-1)), to_x(1))
        copies.send((name, "core", 1), part(buf, at_x(-1)), part(buf, at_x(-1)), sibling)
        copies.wait((name, "left"), part(buf, at_x(1)), to_x(-1))
        copies.send((name, "relay_left"), high(buf, at_x(1)), high(buf, at_x(1)), to_x(-1))
        copies.send((name, "core", 2), part(buf, at_x(1)), part(buf, at_x(1)), sibling)

    def unit_far(name, buf, part, low, high):
        copies.wait((name, "relay_right"), low(buf, at_x(2)), to_x(1))
        copies.wait((name, "relay_left"), high(buf, at_x(2)), to_x(-1))
        copies.send((name, "core", 3), part(buf, at_x(2)), part(buf, at_x(2)), sibling)

    def unit_end(name, buf, part):
        for number, d in enumerate((0, -1, 1, 2)):
            other = ((x + d) % 4) * 2 + 1 - c
            copies.wait((name, "core", number), part(buf, other), sibling)

    def qkv_unit(d):
        shard = at_z(-d)
        return (
            ("wqkv", d),
            wqkv,
            lambda buf, at: buf.at[at, shard],
            lambda buf, at: buf.at[at, shard, pl.ds(0, 96)],
            lambda buf, at: buf.at[at, shard, pl.ds(96, 96)],
        )

    def y_unit(name, buf, d):
        first = at_y(-d) * 4
        return (
            (name, d),
            buf,
            lambda buf, at: buf.at[at, pl.ds(first, 4)],
            lambda buf, at: buf.at[at, pl.ds(first, 2)],
            lambda buf, at: buf.at[at, pl.ds(first + 2, 2)],
        )

    out_units = [y_unit("wout", wout, d) for d in (0, 1, 3, 2)]
    kv_units = [y_unit("wkv", wkv, d) for d in (0, 1, 3, 2)]
    qkv_units = [qkv_unit(d) for d in NEAR_FIRST]

    def over_y(name, buf):
        for d in NEAR_FIRST:
            copies.wait(f"{name}_z{d}", buf.at[q, y * 4 + at_z(-d)], to_z(d))
        part = buf.at[q, pl.ds(y * 4, 4)]
        for d in NEAR_FIRST:
            copies.send((name, "y", d), part, part, to_y(d))

    def from_y(name, buf, units):
        for d, unit in zip(NEAR_FIRST, units[1:]):
            copies.wait((name, "y", d), buf.at[q, pl.ds(at_y(-d) * 4, 4)], to_y(d))
            unit_start(*unit[:3])

    for d, unit in zip(NEAR_FIRST, qkv_units):
        copies.wait(f"wqkv_z{d}", wqkv.at[q, at_z(-d)], to_z(d))
        unit_start(*unit[:3])
    over_y("wout", wout)
    unit_start(*out_units[0][:3])
    for unit in qkv_units:
        unit_relay(*unit)
    over_y("wkv", wkv)
    unit_start(*kv_units[0][:3])
    for unit in qkv_units:
        unit_far(*unit)
    from_y("wout", wout, out_units)

    for number in range(4):
        source = (0, 1, 3, 2)[number]
        for d in NEAR_FIRST:
            shard = at_y(-d) * 4 + at_z(-source)
            copies.wait(("normed", d, number), normed.at[shard], to_y(d))
    for unit in qkv_units:
        unit_end(*unit[:3])

    valid = valid_ref[0]
    key_live = lax.broadcasted_iota(jnp.int32, (256, 256), 1) < valid

    def attend(position):
        here = normed[:, position * 16 : position * 16 + 16, :].reshape(256, D)
        for pair in range(2):
            first = wqkv[:, 2 * pair].reshape(1536, 128)
            second = wqkv[:, 2 * pair + 1].reshape(1536, 128)
            both = jnp.concatenate([first, second], axis=1)
            query_key = dot(here, both[0:1024])
            value_low = dot(here[:, 0:512], both[1024:1536])
            value_high = dot(here[:, 512:1024], both[1024:1536])
            mixed = []
            for head in range(2):
                lo = slice(head * 128, head * 128 + 64)
                hi = slice(head * 128 + 64, head * 128 + 128)
                query = query_key[:, lo].astype(BF16)
                key = query_key[:, hi].astype(BF16)
                value = (value_low[:, lo] + value_high[:, hi]).astype(BF16)
                scores = jnp.where(key_live, dot_nt(query, key) * SCALE, -jnp.inf)
                weights = jnp.exp(scores - jnp.max(scores, axis=-1, keepdims=True))
                total = jnp.sum(weights, axis=-1, keepdims=True)
                mixed.append(dot(weights.astype(BF16), value) / total)
            result = jnp.concatenate(mixed, axis=1).astype(BF16).reshape(4, 4, 16, 128)
            for source in range(4):
                at = source * 32 + position * 16
                att_out[:, at : at + 16, pair * 128 : pair * 128 + 128] = result[:, source]

    attend(0)
    for unit in out_units:
        unit_relay(*unit)
    attend(1)
    for d in NEAR_FIRST:
        copies.send(f"att{d}", att_out.at[at_y(d)], att_in.at[y], to_y(d))
    att_in[y] = att_out[y]
    for unit in out_units:
        unit_far(*unit)
    from_y("wkv", wkv, kv_units)
    for unit in out_units:
        unit_end(*unit[:3])
    for d in NEAR_FIRST:
        copies.wait(f"att{d}", att_in.at[at_y(-d)], to_y(d))

    attended = jnp.concatenate([att_in[source] for source in range(4)], axis=1)
    for block in range(4):
        weight = jnp.concatenate(
            [wout[2 * block].reshape(D, 128), wout[2 * block + 1].reshape(D, 128)], axis=1
        )
        cols = slice(block * 256, block * 256 + 256)
        total = rows[:, :, cols].astype(F32).reshape(128, 256) + dot(attended, weight)
        summed[:, :, cols] = total.astype(BF16).reshape(4, 32, 256)
    for d in NEAR_FIRST:
        copies.send(f"back{d}", summed.at[at_z(d)], back.at[g], to_z(d))
    back[g] = summed[g]

    for unit in kv_units:
        unit_relay(*unit)
    for unit in kv_units:
        unit_far(*unit)

    copies.wait("start_after", start_in.at[0], after)
    copies.wait("start_before", start_in.at[1], before)
    starts_far = jnp.where(lane < 64, start_in[1], start_in[0])[0:1]
    starts_own = start_out[0:1, :]
    row = lax.broadcasted_iota(jnp.int32, (128, 128), 0)
    frame = t * 16 + (row & 15)
    live = [
        (frame >= starts) & (frame < starts + CLIP) & (frame < valid)
        for starts in (starts_own, starts_far)
    ]

    for d in NEAR_FIRST:
        copies.wait(f"back{d}", back.at[at_z(-d)], to_z(d))
    held = back[...].reshape(128, D)
    pooled = layer_norm(held.astype(F32), pool_gain_ref[...]).astype(BF16)
    for half in range(2):
        cols = slice(half * 512, half * 512 + 512)
        temporal_ref[:, cols] = dot(by_frame, held[:, cols]).astype(BF16)
    for unit in kv_units:
        unit_end(*unit[:3])

    def head_queries(head):
        own = [wkv[2 * block, head, 128:144, :] for block in range(4)]
        return jnp.concatenate(own + own, axis=0)[:, 0:64]

    def pool_pair(pair, part_ref, stat_ref):
        weight = jnp.concatenate(
            [
                wkv[:, 2 * pair, 0:128, :].reshape(D, 128),
                wkv[:, 2 * pair + 1, 0:128, :].reshape(D, 128),
            ],
            axis=1,
        )
        pair_kv = dot(pooled, weight)
        for head in range(2):
            own_kv = pair_kv[:, head * 128 : head * 128 + 128]
            key = own_kv[:, 0:64].astype(BF16)
            value_t = jnp.transpose(own_kv)[64:128, :].astype(BF16)
            scores = dot_nt(key, head_queries(2 * pair + head)) * SCALE
            for side in range(2):
                cols = slice(side * 128, side * 128 + 128)
                top = jnp.max(jnp.where(live[side], scores, NEG), axis=0, keepdims=True)
                weights = jnp.where(live[side], jnp.exp(scores - top), 0.0)
                stat_ref[head : head + 1, cols] = top
                stat_ref[head + 2 : head + 3, cols] = jnp.sum(weights, axis=0, keepdims=True)
                part_ref[head * 64 : head * 64 + 64, cols] = dot(
                    value_t, weights.astype(BF16)
                ).astype(BF16)

    stat_out[...] = jnp.zeros_like(stat_out)
    stat_in[q] = jnp.zeros((8, 256), F32)
    for d in range(1, 8):
        to = (q + d) % 8
        pool_pair(to, part_out.at[to], stat_out.at[to])
        copies.send(("part", d), part_out.at[to], part_in.at[q], to_patch(d))
        copies.send(("stat", d), stat_out.at[to], stat_in.at[q], to_patch(d))
    pool_pair(q, part_in.at[q], stat_in.at[q])

    self_scores, self_values = [], []
    for head in range(2):
        weight = wkv[:, 2 * q + head, 0:128, :].reshape(D, 128)
        own_kv = dot(latn[...], weight)
        key = own_kv[:, 0:64].astype(BF16)
        self_values.append(own_kv[:, 64:128].astype(BF16))
        self_scores.append(dot_nt(key, head_queries(2 * q + head)) * SCALE)

    for d in range(1, 8):
        source = (q + 8 - d) % 8
        copies.wait(("part", d), part_in.at[source], to_patch(d))
        copies.wait(("stat", d), stat_in.at[source], to_patch(d))
    tops = [stat_in[source] for source in range(8)]
    highest = tops[0]
    for top in tops[1:]:
        highest = jnp.maximum(highest, top)
    mixes = []
    nstat_out[...] = jnp.zeros_like(nstat_out)
    own_tops, own_totals = [], []
    for head in range(2):
        top = highest[head : head + 1]
        total = jnp.zeros((1, 256), F32)
        mix = jnp.zeros((64, 256), F32)
        for source in range(8):
            factor = jnp.exp(tops[source][head : head + 1] - top)
            total += tops[source][head + 2 : head + 3] * factor
            mix += part_in[source, head * 64 : head * 64 + 64, :].astype(F32) * factor
        own_tops.append(top[:, 0:128])
        own_totals.append(total[:, 0:128])
        mixes.append(mix[:, 0:128])
        near_out[head * 64 : head * 64 + 64, :] = mix[:, 128:256].astype(BF16)
        nstat_out[head : head + 1, :] = top[:, 128:256]
        nstat_out[head + 2 : head + 3, :] = total[:, 128:256]
    copies.send("near_after", near_out, near_in.at[0], after)
    copies.send("nstat_after", nstat_out, nstat_in.at[0], after)
    copies.send("near_before", near_out, near_in.at[1], before)
    copies.send("nstat_before", nstat_out, nstat_in.at[1], before)
    copies.wait("near_after", near_in.at[0], after)
    copies.wait("nstat_after", nstat_in.at[0], after)
    copies.wait("near_before", near_in.at[1], before)
    copies.wait("nstat_before", nstat_in.at[1], before)

    near_stat = jnp.where(lane < 64, nstat_in[0], nstat_in[1])
    wide_lane = lax.broadcasted_iota(jnp.int32, (64, 128), 1)
    results = []
    for head in range(2):
        span = slice(head * 64, head * 64 + 64)
        near_mix = jnp.where(wide_lane < 64, near_in[0, span].astype(F32), near_in[1, span].astype(F32))
        near_top = near_stat[head : head + 1]
        near_total = near_stat[head + 2 : head + 3]
        scores = self_scores[head]
        top = jnp.maximum(
            jnp.maximum(own_tops[head], near_top), jnp.max(scores, axis=0, keepdims=True)
        )
        own_factor = jnp.exp(own_tops[head] - top)
        near_factor = jnp.exp(near_top - top)
        weights = jnp.exp(scores - top)
        total = (
            own_totals[head] * own_factor
            + near_total * near_factor
            + jnp.sum(weights, axis=0, keepdims=True)
        )
        self_mix = lax.dot_general(
            self_values[head],
            weights.astype(BF16),
            (((0,), (0,)), ((), ())),
            preferred_element_type=F32,
        )
        results.append((mixes[head] * own_factor + near_mix * near_factor + self_mix) / total)
    piece = jnp.transpose(jnp.concatenate(results, axis=0)).astype(BF16)
    piece_out[...] = piece
    for d in range(1, 8):
        copies.send(("piece", d), piece_out, piece_in.at[q], to_patch(d))
    piece_in[q] = piece
    for d in range(1, 8):
        copies.wait(("piece", d), piece_in.at[(q + 8 - d) % 8], to_patch(d))
    for block in range(8):
        pooled_ref[:, block * 128 : block * 128 + 128] = piece_in[block]
    copies.drain()
    assert len(copies.slots) <= SLOTS


def on_device(
    tokens,
    frame_gain,
    qkv_weight,
    out_weight,
    pool_gain,
    latent_gain,
    latents,
    query_weight,
    kv_weight,
    clip_starts,
    valid_frames,
):
    frames_dev, patch_dev, width = tokens.shape
    vmem = pl.BlockSpec(memory_space=pltpu.VMEM)
    smem = pl.BlockSpec(memory_space=pltpu.SMEM)
    temporal_out, pooled = pl.pallas_call(
        kernel,
        out_shape=(
            jax.ShapeDtypeStruct((128, D), BF16),
            jax.ShapeDtypeStruct((128, D), BF16),
        ),
        in_specs=[smem, smem] + [vmem] * 9,
        out_specs=(vmem, vmem),
        scratch_shapes=[
            pltpu.VMEM((4, 32, D), BF16),
            pltpu.VMEM((4, 32, D), BF16),
            pltpu.VMEM((16, 32, D), BF16),
            pltpu.VMEM((8, 4, 192, 128), BF16),
            pltpu.VMEM((8, 16, 64, 128), BF16),
            pltpu.VMEM((8, 16, 144, 128), BF16),
            pltpu.VMEM((4, 128, 256), BF16),
            pltpu.VMEM((4, 128, 256), BF16),
            pltpu.VMEM((4, 32, D), BF16),
            pltpu.VMEM((4, 32, D), BF16),
            pltpu.VMEM((64, D), BF16),
            pltpu.VMEM((4, 16, 128), BF16),
            pltpu.VMEM((8, 128), jnp.int32),
            pltpu.VMEM((2, 8, 128), jnp.int32),
            pltpu.VMEM((8, 128, 256), BF16),
            pltpu.VMEM((8, 128, 256), BF16),
            pltpu.VMEM((8, 8, 256), F32),
            pltpu.VMEM((8, 8, 256), F32),
            pltpu.VMEM((128, 128), BF16),
            pltpu.VMEM((2, 128, 128), BF16),
            pltpu.VMEM((8, 128), F32),
            pltpu.VMEM((2, 8, 128), F32),
            pltpu.VMEM((128, 128), BF16),
            pltpu.VMEM((8, 128, 128), BF16),
            pltpu.SemaphoreType.DMA((SLOTS,)),
            pltpu.SemaphoreType.DMA((SLOTS,)),
        ],
        compiler_params=pltpu.CompilerParams(
            collective_id=0, has_side_effects=True, vmem_limit_bytes=48 * 1024 * 1024
        ),
    )(
        clip_starts,
        valid_frames,
        tokens.reshape(frames_dev * patch_dev, width),
        frame_gain.reshape(1, width),
        qkv_weight,
        out_weight,
        pool_gain.reshape(1, width),
        latent_gain.reshape(1, width),
        latents,
        query_weight,
        kv_weight,
    )
    return (
        temporal_out.reshape(frames_dev, patch_dev, width),
        pooled.reshape(2, 64, width),
    )


def solution(mesh):
    in_specs = (
        P(("dp", "tm"), "patch", None),
        P(),
        P(None, "tm"),
        P("tm", None),
        P(),
        P(),
        P(),
        P(None, "tm"),
        P(None, "tm"),
        P(("dp", "tm")),
        P("dp"),
    )
    out_specs = (P(("dp", "tm"), "patch", None), P(("dp", "tm"), None, None))
    return jax.shard_map(
        on_device, mesh=mesh, in_specs=in_specs, out_specs=out_specs, check_vma=False
    )
```

```python
import jax
import jax.numpy as jnp
from jax import lax
from jax.experimental import pallas as pl
from jax.experimental.pallas import tpu as pltpu
from jax.sharding import PartitionSpec as P

MESH = pl.DeviceIdType.MESH
F32 = jnp.float32
BF16 = jnp.bfloat16
D = 1024
HEAD = 64
CLIP = 16
EPS = 1e-05
NEG = -1e30
SCALE = HEAD ** (-0.5)
SLOTS = 160
NEAR_FIRST = (1, 3, 2)


def layer_norm(value, gain):
    center = value - jnp.mean(value, axis=-1, keepdims=True)
    spread = jnp.mean(center * center, axis=-1, keepdims=True)
    return center * lax.rsqrt(spread + EPS) * gain


def dot(a, b):
    return jnp.dot(a, b, preferred_element_type=F32)


def dot_nt(a, b):
    return lax.dot_general(a, b, (((1,), (1,)), ((), ())), preferred_element_type=F32)


class Copies:
    def __init__(self, send_sem, recv_sem):
        self.send_sem = send_sem
        self.recv_sem = recv_sem
        self.slots = {}
        self.started = []

    def slot(self, name):
        return self.slots.setdefault(name, len(self.slots))

    def make(self, name, src, dst, device):
        slot = self.slot(name)
        return pltpu.make_async_remote_copy(
            src_ref=src,
            dst_ref=dst,
            send_sem=self.send_sem.at[slot],
            recv_sem=self.recv_sem.at[slot],
            device_id=device,
            device_id_type=MESH,
        )

    def send(self, name, src, dst, device):
        copy = self.make(name, src, dst, device)
        copy.start()
        self.started.append(copy)

    def wait(self, name, dst, device):
        self.make(name, dst, dst, device).wait_recv()

    def drain(self):
        for copy in self.started:
            copy.wait_send()


def kernel(
    starts_ref,
    valid_ref,
    tokens_ref,
    frame_gain_ref,
    qkv_ref,
    out_w_ref,
    pool_gain_ref,
    latent_gain_ref,
    latents_ref,
    query_w_ref,
    kv_w_ref,
    temporal_ref,
    pooled_ref,
    own_rows,
    rows,
    normed,
    wqkv,
    wout,
    wkv,
    att_out,
    att_in,
    summed,
    back,
    pooled,
    latn,
    held_queries,
    block_queries,
    keys,
    values,
    start_out,
    start_in,
    part_out,
    part_in,
    stat_out,
    stat_in,
    near_out,
    near_in,
    nstat_out,
    nstat_in,
    piece_out,
    piece_in,
    send_sem,
    recv_sem,
):
    t = lax.axis_index("tm")
    q = lax.axis_index("patch")
    y, g = t // 4, t % 4
    x, c = q // 2, q % 2
    copies = Copies(send_sem, recv_sem)

    def at_z(d):
        return (g + d + 4) % 4

    def at_y(d):
        return (y + d + 4) % 4

    def at_x(d):
        return ((x + d + 4) % 4) * 2 + c

    def to_z(d):
        return {"tm": y * 4 + at_z(d)}

    def to_y(d):
        return {"tm": at_y(d) * 4 + g}

    def to_x(d):
        return {"patch": at_x(d)}

    def to_patch(d):
        return {"patch": (q + d) % 8}

    sibling = {"patch": x * 2 + 1 - c}
    after = {"tm": (t + 1) % 16}
    before = {"tm": (t + 15) % 16}

    barrier = pltpu.get_barrier_semaphore()
    partners = (
        [to_z(d) for d in (1, 2, 3)]
        + [to_y(d) for d in (1, 2, 3)]
        + [to_patch(d) for d in range(1, 8)]
        + [after, before]
    )
    for partner in partners:
        pl.semaphore_signal(barrier, inc=1, device_id=partner, device_id_type=MESH)

    to_row = lax.broadcasted_iota(jnp.int32, (128, 128), 0)
    from_row = lax.broadcasted_iota(jnp.int32, (128, 128), 1)
    by_position = jnp.where(from_row == (to_row & 15) * 8 + (to_row >> 4), 1.0, 0.0).astype(BF16)
    for half in range(2):
        cols = slice(half * 512, half * 512 + 512)
        own_rows[:, :, cols] = dot(by_position, tokens_ref[:, cols]).astype(BF16).reshape(4, 32, 512)
    for block in range(8):
        wqkv[block, g] = qkv_ref[:, block * 128 : block * 128 + 128]

    pl.semaphore_wait(barrier, len(partners))

    for d in NEAR_FIRST:
        copies.send(f"wqkv_z{d}", wqkv.at[q, g], wqkv.at[q, g], to_z(d))
    for d in NEAR_FIRST:
        copies.send(f"rows{d}", own_rows.at[at_z(d)], rows.at[g], to_z(d))

    lane = lax.broadcasted_iota(jnp.int32, (8, 128), 1)
    start_out[...] = jnp.where(lane < 64, starts_ref[0], starts_ref[1])
    copies.send("start_after", start_out, start_in.at[0], after)
    copies.send("start_before", start_out, start_in.at[1], before)

    frame_gain = frame_gain_ref[...]

    def spread_rows(number, source):
        shard = y * 4 + source
        normed[shard] = layer_norm(rows[source].astype(F32), frame_gain).astype(BF16)
        for d in NEAR_FIRST:
            copies.send(("normed", d, number), normed.at[shard], normed.at[shard], to_y(d))

    rows[g] = own_rows[g]
    spread_rows(0, g)

    eighth = pl.ds(pl.multiple_of(q * 128, 128), 128)
    wout[q, t] = out_w_ref[:, eighth]

    latn[...] = layer_norm(latents_ref[...].astype(F32), latent_gain_ref[...]).astype(BF16)
    queries = dot_nt(query_w_ref[...], latn[...])
    held_queries[...] = jnp.concatenate([queries, queries], axis=1).astype(BF16).reshape(4, 16, 128)
    wkv[q, t, 0:128, :] = jnp.transpose(kv_w_ref[eighth, :].astype(F32)).astype(BF16)
    wkv[q, t, 128:144, :] = held_queries[q // 2]

    def unit_start(name, buf, part):
        copies.send((name, "right"), part(buf, q), part(buf, q), to_x(1))
        copies.send((name, "left"), part(buf, q), part(buf, q), to_x(-1))
        copies.send((name, "core", 0), part(buf, q), part(buf, q), sibling)

    def unit_relay(name, buf, part, low, high):
        copies.wait((name, "right"), part(buf, at_x(-1)), to_x(1))
        copies.send((name, "relay_right"), low(buf, at_x(-1)), low(buf, at_x(-1)), to_x(1))
        copies.send((name, "core", 1), part(buf, at_x(-1)), part(buf, at_x(-1)), sibling)
        copies.wait((name, "left"), part(buf, at_x(1)), to_x(-1))
        copies.send((name, "relay_left"), high(buf, at_x(1)), high(buf, at_x(1)), to_x(-1))
        copies.send((name, "core", 2), part(buf, at_x(1)), part(buf, at_x(1)), sibling)

    def unit_far(name, buf, part, low, high):
        copies.wait((name, "relay_right"), low(buf, at_x(2)), to_x(1))
        copies.wait((name, "relay_left"), high(buf, at_x(2)), to_x(-1))
        copies.send((name, "core", 3), part(buf, at_x(2)), part(buf, at_x(2)), sibling)

    def unit_end(name, buf, part):
        for number, d in enumerate((0, -1, 1, 2)):
            other = ((x + d + 4) % 4) * 2 + 1 - c
            copies.wait((name, "core", number), part(buf, other), sibling)

    def qkv_unit(d):
        shard = at_z(-d)
        return (
            ("wqkv", d),
            wqkv,
            lambda buf, at: buf.at[at, shard],
            lambda buf, at: buf.at[at, shard, pl.ds(0, 96)],
            lambda buf, at: buf.at[at, shard, pl.ds(96, 96)],
        )

    def y_unit(name, buf, d):
        first = at_y(-d) * 4
        return (
            (name, d),
            buf,
            lambda buf, at: buf.at[at, pl.ds(first, 4)],
            lambda buf, at: buf.at[at, pl.ds(first, 2)],
            lambda buf, at: buf.at[at, pl.ds(first + 2, 2)],
        )

    out_units = [y_unit("wout", wout, d) for d in (0, 1, 3, 2)]
    kv_units = [y_unit("wkv", wkv, d) for d in (0, 1, 3, 2)]
    qkv_units = [qkv_unit(d) for d in NEAR_FIRST]

    def over_z(name, buf):
        for d in NEAR_FIRST:
            copies.send(f"{name}_z{d}", buf.at[q, t], buf.at[q, t], to_z(d))

    def over_y(name, buf):
        for d in NEAR_FIRST:
            copies.wait(f"{name}_z{d}", buf.at[q, y * 4 + at_z(-d)], to_z(d))
        part = buf.at[q, pl.ds(y * 4, 4)]
        for d in NEAR_FIRST:
            copies.send((name, "y", d), part, part, to_y(d))

    def from_y(name, buf, units):
        for d, unit in zip(NEAR_FIRST, units[1:]):
            copies.wait((name, "y", d), buf.at[q, pl.ds(at_y(-d) * 4, 4)], to_y(d))
            unit_start(*unit[:3])

    for d, unit in zip(NEAR_FIRST, qkv_units):
        copies.wait(f"wqkv_z{d}", wqkv.at[q, at_z(-d)], to_z(d))
        unit_start(*unit[:3])
    for number, d in ((1, 1), (2, 3)):
        copies.wait(f"rows{d}", rows.at[at_z(-d)], to_z(d))
        spread_rows(number, at_z(-d))
    for unit in qkv_units:
        unit_relay(*unit)
    copies.wait("rows2", rows.at[at_z(-2)], to_z(2))
    spread_rows(3, at_z(-2))
    over_z("wout", wout)
    over_z("wkv", wkv)
    for unit in qkv_units:
        unit_far(*unit)
    for number, source in enumerate((0, 1, 3, 2)):
        for d in NEAR_FIRST:
            shard = at_y(-d) * 4 + at_z(-source)
            copies.wait(("normed", d, number), normed.at[shard], to_y(d))
    for unit in qkv_units:
        unit_end(*unit[:3])

    valid = valid_ref[0]
    key_live = lax.broadcasted_iota(jnp.int32, (256, 256), 1) < valid
    first_head = lax.broadcasted_iota(jnp.int32, (256, 128), 1) < 64

    def attend(position):
        here = normed[:, position * 16 : position * 16 + 16, :].reshape(256, D)
        for pair in range(2):
            blocks = []
            for block in range(8):
                parts = [
                    wqkv[block, 2 * pair + head, kind * 64 : kind * 64 + 64, :]
                    for kind in range(3)
                    for head in range(2)
                ]
                blocks.append(jnp.concatenate(parts, axis=0))
            weight = jnp.concatenate(blocks, axis=1)
            projected = dot_nt(here, weight).astype(BF16)
            query, key, value = (projected[:, k * 128 : k * 128 + 128] for k in range(3))
            mixed = []
            for head in range(2):
                mine = first_head if head == 0 else jnp.logical_not(first_head)
                scores = dot_nt(jnp.where(mine, query, jnp.zeros_like(query)), key) * SCALE
                scores = jnp.where(key_live, scores, -jnp.inf)
                weights = jnp.exp(scores - jnp.max(scores, axis=-1, keepdims=True))
                total = jnp.sum(weights, axis=-1, keepdims=True)
                mixed.append(dot(weights.astype(BF16), value) / total)
            result = jnp.where(first_head, mixed[0], mixed[1]).astype(BF16)
            att_out[position, :, :, pair * 128 : pair * 128 + 128] = result.reshape(4, 64, 128)
        for d in NEAR_FIRST:
            copies.send(
                ("att", d, position), att_out.at[position, at_y(d)], att_in.at[position, y], to_y(d)
            )
        att_in[position, y] = att_out[position, y]

    def project(position):
        for d in NEAR_FIRST:
            copies.wait(("att", d, position), att_in.at[position, at_y(-d)], to_y(d))
        attended = jnp.concatenate([att_in[position, source] for source in range(4)], axis=1)
        for block in range(4):
            weight = jnp.concatenate(
                [wout[2 * block].reshape(D, 128), wout[2 * block + 1].reshape(D, 128)], axis=1
            )
            cols = slice(block * 256, block * 256 + 256)
            tokens = rows[:, position * 16 : position * 16 + 16, cols]
            total = tokens.astype(F32).reshape(64, 256) + dot(attended, weight)
            summed[position, :, :, cols] = total.astype(BF16).reshape(4, 16, 256)
        for d in NEAR_FIRST:
            copies.send(
                ("back", d, position), summed.at[position, at_z(d)], back.at[position, g], to_z(d)
            )
        back[position, g] = summed[position, g]

    attend(0)
    over_y("wout", wout)
    unit_start(*out_units[0][:3])
    attend(1)
    over_y("wkv", wkv)
    unit_start(*kv_units[0][:3])
    from_y("wout", wout, out_units)
    for unit in out_units:
        unit_relay(*unit)
    from_y("wkv", wkv, kv_units)
    for unit in out_units:
        unit_far(*unit)
    for unit in out_units:
        unit_end(*unit[:3])
    project(0)
    project(1)

    for unit in kv_units:
        unit_relay(*unit)
    for unit in kv_units:
        unit_far(*unit)
    copies.wait("start_after", start_in.at[0], after)
    copies.wait("start_before", start_in.at[1], before)

    pool_gain = pool_gain_ref[...]

    def pool_norm(position, source):
        value = layer_norm(back[position, source].astype(F32), pool_gain)
        pooled[position, source] = value.astype(BF16)

    for position in range(2):
        pool_norm(position, g)
        for d in NEAR_FIRST:
            copies.wait(("back", d, position), back.at[position, at_z(-d)], to_z(d))
            pool_norm(position, at_z(-d))
    for unit in kv_units:
        unit_end(*unit[:3])

    wide_lane = lax.broadcasted_iota(jnp.int32, (64, 256), 1)
    for quad in range(4):
        for head in range(4):
            parts = [wkv[2 * block, 4 * quad + head, 128:144, :] for block in range(4)]
            query = jnp.concatenate(parts, axis=0)
            query = jnp.concatenate([query, query], axis=1)
            block_queries[quad, head * 64 : head * 64 + 64, :] = jnp.where(
                (wide_lane >> 6) == head, query, jnp.zeros_like(query)
            )

    far_starts = jnp.where(lane < 64, start_in[1], start_in[0])[0:1]
    own_starts = start_out[0:1, :]
    frame = t * 16 + (lax.broadcasted_iota(jnp.int32, (128, 128), 0) & 15)
    in_lane = lax.broadcasted_iota(jnp.int32, (1, 128), 1)

    def live_of(starts, second):
        half = jnp.where((in_lane >= 64) == second, starts, -(10**6))
        start = jnp.max(half, axis=1, keepdims=True)
        return (frame >= start) & (frame < start + CLIP) & (frame < valid)

    live = [
        live_of(own_starts, False),
        live_of(own_starts, True),
        live_of(far_starts, False),
        live_of(far_starts, True),
    ]
    live = [jnp.concatenate([mask, mask], axis=1) for mask in live]
    pair_lane = lax.broadcasted_iota(jnp.int32, (64, 128), 1)
    rows_now = pooled[...].reshape(128, D)

    def kv_project(quad):
        key_blocks, value_blocks = [], []
        for block in range(8):
            four = wkv[block, pl.ds(quad * 4, 4)]
            key_blocks.append(four[:, 0:64, :].reshape(256, 128))
            value_blocks.append(four[:, 64:128, :].reshape(256, 128))
        keys[quad] = dot_nt(rows_now, jnp.concatenate(key_blocks, axis=1)).astype(BF16)
        values[quad] = dot_nt(jnp.concatenate(value_blocks, axis=1), rows_now).astype(BF16)

    def pool_quad(quad):
        scores = dot(keys[quad], block_queries[quad]) * SCALE
        value = values[quad]
        for clip in range(4):
            top = jnp.max(jnp.where(live[clip], scores, NEG), axis=0, keepdims=True)
            weights = jnp.where(live[clip], jnp.exp(scores - top), 0.0)
            total = jnp.sum(weights, axis=0, keepdims=True)
            mix = dot(value, weights.astype(BF16))
            for pair in range(2):
                cols = slice(pair * 128, pair * 128 + 128)
                even = mix[pair * 128 : pair * 128 + 64, cols]
                odd = mix[pair * 128 + 64 : pair * 128 + 128, cols]
                part_out[quad, pair, clip * 64 : clip * 64 + 64, :] = jnp.where(
                    pair_lane < 64, even, odd
                ).astype(BF16)
                stat_out[quad, pair, clip : clip + 1, :] = top[:, cols]
                stat_out[quad, pair, 4 + clip : 5 + clip, :] = total[:, cols]

    def send_part(name, quad, core):
        device = {"patch": quad * 2 + core}
        copies.send(("part", name), part_out.at[quad, core], part_in.at[q], device)
        copies.send(("stat", name), stat_out.at[quad, core], stat_in.at[q], device)

    order = [(x + k) % 4 for k in (2, 1, 3, 0)]
    kv_project(order[0])
    for number, quad in enumerate(order):
        if number < 3:
            kv_project(order[number + 1])
        pool_quad(quad)
        if number < 3:
            send_part(("same", number), quad, c)
        send_part(("cross", number), quad, 1 - c)
    part_in[q] = part_out[x, c]
    stat_in[q] = stat_out[x, c]

    key_blocks, value_blocks = [], []
    for block in range(8):
        two = wkv[block, pl.ds(q * 2, 2)]
        key_blocks.append(two[:, 0:64, :].reshape(128, 128))
        value_blocks.append(two[:, 64:128, :].reshape(128, 128))
    self_key = dot_nt(latn[...], jnp.concatenate(key_blocks, axis=1)).astype(BF16)
    self_value = dot_nt(jnp.concatenate(value_blocks, axis=1), latn[...]).astype(BF16)
    pair_queries = jnp.where(
        c == 0, block_queries[x, 0:128, 0:128], block_queries[x, 128:256, 128:256]
    )
    self_scores = dot(self_key, pair_queries) * SCALE
    self_top = jnp.max(self_scores, axis=0, keepdims=True)

    by_frame = jnp.where(
        from_row == (to_row & 1) * 64 + ((to_row & 7) >> 1) * 16 + (to_row >> 3), 1.0, 0.0
    ).astype(BF16)
    held = back[...].reshape(128, D)
    for half in range(2):
        cols = slice(half * 512, half * 512 + 512)
        temporal_ref[:, cols] = dot(by_frame, held[:, cols]).astype(BF16)

    for number, k in enumerate((2, 1, 3, 0)):
        source = ((x + 4 - k) % 4) * 2
        if number < 3:
            copies.wait(("part", ("same", number)), part_in.at[source + c], to_x(k))
            copies.wait(("stat", ("same", number)), stat_in.at[source + c], to_x(k))
        copies.wait(("part", ("cross", number)), part_in.at[source + 1 - c], sibling)
        copies.wait(("stat", ("cross", number)), stat_in.at[source + 1 - c], sibling)
    stats = [stat_in[source] for source in range(8)]
    highest = stats[0][0:4]
    for stat in stats[1:]:
        highest = jnp.maximum(highest, stat[0:4])
    factors = [jnp.exp(stat[0:4] - highest) for stat in stats]
    totals = jnp.zeros((4, 128), F32)
    for stat, factor in zip(stats, factors):
        totals += stat[4:8] * factor
    nstat_out[0:4, :] = highest
    nstat_out[4:8, :] = totals

    def gathered(clip):
        mix = jnp.zeros((64, 128), F32)
        for source in range(8):
            part = part_in[source, clip * 64 : clip * 64 + 64, :].astype(F32)
            mix += part * factors[source][clip : clip + 1]
        return mix

    near_out[0] = gathered(2).astype(BF16)
    copies.send("near_after", near_out.at[0], near_in.at[0], after)
    copies.send("nstat_after", nstat_out, nstat_in.at[0], after)
    near_out[1] = gathered(3).astype(BF16)
    copies.send("near_before", near_out.at[1], near_in.at[1], before)
    copies.send("nstat_before", nstat_out, nstat_in.at[1], before)
    own_mixes = [gathered(0), gathered(1)]

    finished = []
    for clip, name, device in ((0, "after", after), (1, "before", before)):
        copies.wait(f"near_{name}", near_in.at[clip], device)
        copies.wait(f"nstat_{name}", nstat_in.at[clip], device)
        near_top = nstat_in[clip, 2 + clip : 3 + clip, :]
        near_total = nstat_in[clip, 6 + clip : 7 + clip, :]
        own_top = highest[clip : clip + 1]
        top = jnp.maximum(jnp.maximum(own_top, near_top), self_top)
        own_factor = jnp.exp(own_top - top)
        near_factor = jnp.exp(near_top - top)
        weights = jnp.exp(self_scores - top)
        total = (
            totals[clip : clip + 1] * own_factor
            + near_total * near_factor
            + jnp.sum(weights, axis=0, keepdims=True)
        )
        self_mix = dot(self_value, weights.astype(BF16))
        self_mix = jnp.where(pair_lane < 64, self_mix[0:64], self_mix[64:128])
        mix = own_mixes[clip] * own_factor + near_in[clip].astype(F32) * near_factor + self_mix
        finished.append(mix / total)

    turned = jnp.transpose(jnp.concatenate(finished, axis=0))
    even, odd = turned[0:64], turned[64:128]
    piece_out[0:64, :] = jnp.where(pair_lane < 64, even, pltpu.roll(odd, 64, 1)).astype(BF16)
    piece_out[64:128, :] = jnp.where(pair_lane < 64, pltpu.roll(even, 64, 1), odd).astype(BF16)
    for d in range(1, 8):
        copies.send(("piece", d), piece_out, piece_in.at[q], to_patch(d))
    piece_in[q] = piece_out[...]
    for d in range(1, 8):
        copies.wait(("piece", d), piece_in.at[(q + 8 - d) % 8], to_patch(d))
    for block in range(8):
        pooled_ref[:, block * 128 : block * 128 + 128] = piece_in[block]
    copies.drain()
    assert len(copies.slots) <= SLOTS


def on_device(
    tokens,
    frame_gain,
    qkv_weight,
    out_weight,
    pool_gain,
    latent_gain,
    latents,
    query_weight,
    kv_weight,
    clip_starts,
    valid_frames,
):
    frames_dev, patch_dev, width = tokens.shape
    vmem = pl.BlockSpec(memory_space=pltpu.VMEM)
    smem = pl.BlockSpec(memory_space=pltpu.SMEM)
    temporal_out, pooled = pl.pallas_call(
        kernel,
        out_shape=(
            jax.ShapeDtypeStruct((128, D), BF16),
            jax.ShapeDtypeStruct((128, D), BF16),
        ),
        in_specs=[smem, smem] + [vmem] * 9,
        out_specs=(vmem, vmem),
        scratch_shapes=[
            pltpu.VMEM((4, 32, D), BF16),
            pltpu.VMEM((4, 32, D), BF16),
            pltpu.VMEM((16, 32, D), BF16),
            pltpu.VMEM((8, 4, 192, 128), BF16),
            pltpu.VMEM((8, 16, 64, 128), BF16),
            pltpu.VMEM((8, 16, 144, 128), BF16),
            pltpu.VMEM((2, 4, 64, 256), BF16),
            pltpu.VMEM((2, 4, 64, 256), BF16),
            pltpu.VMEM((2, 4, 16, D), BF16),
            pltpu.VMEM((2, 4, 16, D), BF16),
            pltpu.VMEM((2, 4, 16, D), BF16),
            pltpu.VMEM((64, D), BF16),
            pltpu.VMEM((4, 16, 128), BF16),
            pltpu.VMEM((4, 256, 256), BF16),
            pltpu.VMEM((4, 128, 256), BF16),
            pltpu.VMEM((4, 256, 128), BF16),
            pltpu.VMEM((8, 128), jnp.int32),
            pltpu.VMEM((2, 8, 128), jnp.int32),
            pltpu.VMEM((4, 2, 256, 128), BF16),
            pltpu.VMEM((8, 256, 128), BF16),
            pltpu.VMEM((4, 2, 8, 128), F32),
            pltpu.VMEM((8, 8, 128), F32),
            pltpu.VMEM((2, 64, 128), BF16),
            pltpu.VMEM((2, 64, 128), BF16),
            pltpu.VMEM((8, 128), F32),
            pltpu.VMEM((2, 8, 128), F32),
            pltpu.VMEM((128, 128), BF16),
            pltpu.VMEM((8, 128, 128), BF16),
            pltpu.SemaphoreType.DMA((SLOTS,)),
            pltpu.SemaphoreType.DMA((SLOTS,)),
        ],
        compiler_params=pltpu.CompilerParams(
            collective_id=0, has_side_effects=True, vmem_limit_bytes=48 * 1024 * 1024
        ),
    )(
        clip_starts,
        valid_frames,
        tokens.reshape(frames_dev * patch_dev, width),
        frame_gain.reshape(1, width),
        qkv_weight.T,
        out_weight,
        pool_gain.reshape(1, width),
        latent_gain.reshape(1, width),
        latents,
        query_weight.T,
        kv_weight,
    )
    return (
        temporal_out.reshape(frames_dev, patch_dev, width),
        pooled.reshape(2, 64, width),
    )


def solution(mesh):
    in_specs = (
        P(("dp", "tm"), "patch", None),
        P(),
        P(None, "tm"),
        P("tm", None),
        P(),
        P(),
        P(),
        P(None, "tm"),
        P(None, "tm"),
        P(("dp", "tm")),
        P("dp"),
    )
    out_specs = (P(("dp", "tm"), "patch", None), P(("dp", "tm"), None, None))
    return jax.shard_map(
        on_device, mesh=mesh, in_specs=in_specs, out_specs=out_specs, check_vma=False
    )
```

```python
import jax
import jax.numpy as jnp
from jax import lax
from jax.experimental import pallas as pl
from jax.experimental.pallas import tpu as pltpu
from jax.sharding import PartitionSpec as P

MESH = pl.DeviceIdType.MESH
F32 = jnp.float32
BF16 = jnp.bfloat16
D = 1024
HEAD = 64
CLIP = 16
EPS = 1e-05
NEG = -1e30
SCALE = HEAD ** (-0.5)
SLOTS = 200
NEAR_FIRST = (1, 3, 2)


def layer_norm(value, gain):
    center = value - jnp.mean(value, axis=-1, keepdims=True)
    spread = jnp.mean(center * center, axis=-1, keepdims=True)
    return center * lax.rsqrt(spread + EPS) * gain


def dot(a, b):
    return jnp.dot(a, b, preferred_element_type=F32)


def dot_nt(a, b):
    return lax.dot_general(a, b, (((1,), (1,)), ((), ())), preferred_element_type=F32)


class Copies:
    def __init__(self, send_sem, recv_sem):
        self.send_sem = send_sem
        self.recv_sem = recv_sem
        self.slots = {}
        self.started = []

    def slot(self, name):
        return self.slots.setdefault(name, len(self.slots))

    def make(self, name, src, dst, device):
        slot = self.slot(name)
        return pltpu.make_async_remote_copy(
            src_ref=src,
            dst_ref=dst,
            send_sem=self.send_sem.at[slot],
            recv_sem=self.recv_sem.at[slot],
            device_id=device,
            device_id_type=MESH,
        )

    def send(self, name, src, dst, device):
        copy = self.make(name, src, dst, device)
        copy.start()
        self.started.append(copy)

    def wait(self, name, dst, device):
        self.make(name, dst, dst, device).wait_recv()

    def drain(self, count=None):
        done, self.started = self.started[:count], self.started[len(self.started[:count]) :]
        for copy in done:
            copy.wait_send()


def kernel(
    starts_hbm,
    valid_hbm,
    tokens_hbm,
    frame_gain_hbm,
    qkv_hbm,
    out_w_hbm,
    pool_gain_hbm,
    latent_gain_hbm,
    latents_hbm,
    query_w_hbm,
    kv_w_hbm,
    temporal_ref,
    pooled_ref,
    starts_ref,
    valid_ref,
    tokens_ref,
    frame_gain_ref,
    pool_gain_ref,
    latent_gain_ref,
    latents_ref,
    query_w_ref,
    kv_w_ref,
    own_rows,
    rows,
    normed,
    wqkv,
    wout,
    wkv,
    att_out,
    att_in,
    summed,
    back,
    pooled,
    latn,
    held_queries,
    block_queries,
    scores_at,
    values,
    start_out,
    start_in,
    part_out,
    part_in,
    stat_out,
    stat_in,
    near_out,
    near_in,
    nstat_out,
    nstat_in,
    piece_out,
    piece_in,
    load_sem,
    send_sem,
    recv_sem,
):
    t = lax.axis_index("tm")
    q = lax.axis_index("patch")
    y, g = t // 4, t % 4
    x, c = q // 2, q % 2
    copies = Copies(send_sem, recv_sem)

    def at_z(d):
        return (g + d + 4) % 4

    def at_y(d):
        return (y + d + 4) % 4

    def at_x(d):
        return ((x + d + 4) % 4) * 2 + c

    def to_z(d):
        return {"tm": y * 4 + at_z(d)}

    def to_y(d):
        return {"tm": at_y(d) * 4 + g}

    def to_x(d):
        return {"patch": at_x(d)}

    def to_patch(d):
        return {"patch": (q + d) % 8}

    sibling = {"patch": x * 2 + 1 - c}
    after = {"tm": (t + 1) % 16}
    before = {"tm": (t + 15) % 16}

    barrier = pltpu.get_barrier_semaphore()
    partners = (
        [to_z(d) for d in (1, 2, 3)]
        + [to_y(d) for d in (1, 2, 3)]
        + [to_patch(d) for d in range(1, 8)]
        + [after, before]
    )
    for partner in partners:
        pl.semaphore_signal(barrier, inc=1, device_id=partner, device_id_type=MESH)

    eighth = pl.ds(pl.multiple_of(q * 128, 128), 128)
    loads = [
        pltpu.make_async_copy(src, dst, load_sem.at[number])
        for number, (src, dst) in enumerate(
            [(tokens_hbm, tokens_ref)]
            + [(qkv_hbm.at[:, pl.ds(b * 128, 128)], wqkv.at[b, g]) for b in range(8)]
            + [
                (out_w_hbm.at[:, eighth], wout.at[q, t]),
                (frame_gain_hbm, frame_gain_ref),
                (latents_hbm, latents_ref),
                (latent_gain_hbm, latent_gain_ref),
                (query_w_hbm, query_w_ref),
                (kv_w_hbm.at[eighth, :], kv_w_ref),
                (pool_gain_hbm, pool_gain_ref),
                (starts_hbm, starts_ref),
                (valid_hbm, valid_ref),
            ]
        )
    ]
    for load in loads:
        load.start()

    to_row = lax.broadcasted_iota(jnp.int32, (128, 128), 0)
    from_row = lax.broadcasted_iota(jnp.int32, (128, 128), 1)
    by_position = jnp.where(
        from_row == (to_row & 15) * 8 + ((to_row >> 4) & 3) * 2 + (to_row >> 6), 1.0, 0.0
    ).astype(BF16)
    loads[0].wait()
    for half in range(2):
        cols = slice(half * 512, half * 512 + 512)
        moved = dot(by_position, tokens_ref[:, cols]).astype(BF16)
        own_rows[:, :, :, cols] = moved.reshape(2, 4, 16, 512)
    for load in loads[1:10]:
        load.wait()

    pl.semaphore_wait(barrier, len(partners))

    for d in NEAR_FIRST:
        copies.send(f"wqkv_z{d}", wqkv.at[q, g], wqkv.at[q, g], to_z(d))
    for d in NEAR_FIRST:
        copies.send(f"wout_z{d}", wout.at[q, t], wout.at[q, t], to_z(d))
    def send_rows(position):
        for d in NEAR_FIRST:
            copies.send(
                ("rows", d, position),
                own_rows.at[position, at_z(d)],
                rows.at[position, g],
                to_z(d),
            )

    send_rows(0)
    send_rows(1)

    for load in loads[10:]:
        load.wait()
    lane = lax.broadcasted_iota(jnp.int32, (8, 128), 1)
    start_out[...] = jnp.where(lane < 64, starts_ref[0], starts_ref[1])
    copies.send("start_after", start_out, start_in.at[0], after)
    copies.send("start_before", start_out, start_in.at[1], before)

    frame_gain = frame_gain_ref[...]

    def spread_rows(position, number, source):
        shard = y * 4 + source
        value = layer_norm(rows[position, source].astype(F32), frame_gain)
        normed[position, shard] = value.astype(BF16)
        part = normed.at[position, shard]
        for d in NEAR_FIRST:
            copies.send(("normed", d, position, number), part, part, to_y(d))

    def receive_rows(position):
        for number, d in ((1, 1), (2, 3), (3, 2)):
            copies.wait(("rows", d, position), rows.at[position, at_z(-d)], to_z(d))
            spread_rows(position, number, at_z(-d))

    def receive_normed(position):
        for number, source in enumerate((0, 1, 3, 2)):
            for d in NEAR_FIRST:
                shard = at_y(-d) * 4 + at_z(-source)
                copies.wait(("normed", d, position, number), normed.at[position, shard], to_y(d))

    for position in range(2):
        rows[position, g] = own_rows[position, g]
        spread_rows(position, 0, g)

    latn[...] = layer_norm(latents_ref[...].astype(F32), latent_gain_ref[...]).astype(BF16)
    queries = dot_nt(query_w_ref[...], latn[...])
    held_queries[...] = jnp.concatenate([queries, queries], axis=1).astype(BF16).reshape(4, 16, 128)
    wkv[q, t, 0:128, :] = jnp.transpose(kv_w_ref[...].astype(F32)).astype(BF16)
    wkv[q, t, 128:144, :] = held_queries[q // 2]

    def unit_start(name, buf, part):
        copies.send((name, "right"), part(buf, q), part(buf, q), to_x(1))
        copies.send((name, "left"), part(buf, q), part(buf, q), to_x(-1))
        copies.send((name, "core", 0), part(buf, q), part(buf, q), sibling)

    def unit_relay(name, buf, part, low, high):
        copies.wait((name, "right"), part(buf, at_x(-1)), to_x(1))
        copies.send((name, "relay_right"), low(buf, at_x(-1)), low(buf, at_x(-1)), to_x(1))
        copies.send((name, "core", 1), part(buf, at_x(-1)), part(buf, at_x(-1)), sibling)
        copies.wait((name, "left"), part(buf, at_x(1)), to_x(-1))
        copies.send((name, "relay_left"), high(buf, at_x(1)), high(buf, at_x(1)), to_x(-1))
        copies.send((name, "core", 2), part(buf, at_x(1)), part(buf, at_x(1)), sibling)

    def unit_far(name, buf, part, low, high):
        copies.wait((name, "relay_right"), low(buf, at_x(2)), to_x(1))
        copies.wait((name, "relay_left"), high(buf, at_x(2)), to_x(-1))
        copies.send((name, "core", 3), part(buf, at_x(2)), part(buf, at_x(2)), sibling)

    def unit_end(name, buf, part):
        for number, d in enumerate((0, -1, 1, 2)):
            other = ((x + d + 4) % 4) * 2 + 1 - c
            copies.wait((name, "core", number), part(buf, other), sibling)

    def qkv_unit(d):
        shard = at_z(-d)
        return (
            ("wqkv", d),
            wqkv,
            lambda buf, at: buf.at[at, shard],
            lambda buf, at: buf.at[at, shard, pl.ds(0, 96)],
            lambda buf, at: buf.at[at, shard, pl.ds(96, 96)],
        )

    def y_unit(name, buf, d):
        first = at_y(-d) * 4
        return (
            (name, d),
            buf,
            lambda buf, at: buf.at[at, pl.ds(first, 4)],
            lambda buf, at: buf.at[at, pl.ds(first, 2)],
            lambda buf, at: buf.at[at, pl.ds(first + 2, 2)],
        )

    out_units = [y_unit("wout", wout, d) for d in (0, 1, 3, 2)]
    qkv_units = [qkv_unit(d) for d in NEAR_FIRST]

    def over_y(name, buf):
        for d in NEAR_FIRST:
            copies.wait(f"{name}_z{d}", buf.at[q, y * 4 + at_z(-d)], to_z(d))
        part = buf.at[q, pl.ds(y * 4, 4)]
        for d in NEAR_FIRST:
            copies.send((name, "y", d), part, part, to_y(d))

    def from_y(name, buf, units):
        for d, unit in zip(NEAR_FIRST, units[1:]):
            copies.wait((name, "y", d), buf.at[q, pl.ds(at_y(-d) * 4, 4)], to_y(d))
            unit_start(*unit[:3])

    for d, unit in zip(NEAR_FIRST, qkv_units):
        copies.wait(f"wqkv_z{d}", wqkv.at[q, at_z(-d)], to_z(d))
        unit_start(*unit[:3])
    over_y("wout", wout)
    unit_start(*out_units[0][:3])
    receive_rows(0)
    for unit in qkv_units:
        unit_relay(*unit)
    for d in NEAR_FIRST:
        copies.send(f"wkv_z{d}", wkv.at[q, t], wkv.at[q, t], to_z(d))
    receive_rows(1)
    for unit in qkv_units:
        unit_far(*unit)
    from_y("wout", wout, out_units)
    receive_normed(0)
    for unit in qkv_units:
        unit_end(*unit[:3])
    early = len(copies.started)

    valid = valid_ref[0]
    key_live = lax.broadcasted_iota(jnp.int32, (256, 256), 1) < valid
    first_head = lax.broadcasted_iota(jnp.int32, (256, 128), 1) < 64

    def attend(position):
        here = normed[position].reshape(256, D)
        for pair in range(2):
            blocks = []
            for block in range(8):
                parts = [
                    wqkv[block, 2 * pair + head, kind * 64 : kind * 64 + 64, :]
                    for kind in range(3)
                    for head in range(2)
                ]
                blocks.append(jnp.concatenate(parts, axis=0))
            weight = jnp.concatenate(blocks, axis=1)
            projected = dot_nt(here, weight).astype(BF16)
            query, key, value = (projected[:, k * 128 : k * 128 + 128] for k in range(3))
            mixed = []
            for head in range(2):
                mine = first_head if head == 0 else jnp.logical_not(first_head)
                scores = dot_nt(jnp.where(mine, query, jnp.zeros_like(query)), key) * SCALE
                scores = jnp.where(key_live, scores, -jnp.inf)
                weights = jnp.exp(scores - jnp.max(scores, axis=-1, keepdims=True))
                total = jnp.sum(weights, axis=-1, keepdims=True)
                mixed.append(dot(weights.astype(BF16), value) / total)
            result = jnp.where(first_head, mixed[0], mixed[1]).astype(BF16)
            att_out[position, :, :, pair * 128 : pair * 128 + 128] = result.reshape(4, 64, 128)
        for d in NEAR_FIRST:
            copies.send(
                ("att", d, position), att_out.at[position, at_y(d)], att_in.at[position, y], to_y(d)
            )
        att_in[position, y] = att_out[position, y]

    def project(position):
        for d in NEAR_FIRST:
            copies.wait(("att", d, position), att_in.at[position, at_y(-d)], to_y(d))
        attended = jnp.concatenate([att_in[position, source] for source in range(4)], axis=1)
        for block in range(4):
            weight = jnp.concatenate(
                [wout[2 * block].reshape(D, 128), wout[2 * block + 1].reshape(D, 128)], axis=1
            )
            cols = slice(block * 256, block * 256 + 256)
            tokens = rows[position, :, :, cols]
            total = tokens.astype(F32).reshape(64, 256) + dot(attended, weight)
            summed[position, :, :, cols] = total.astype(BF16).reshape(4, 16, 256)
        for d in NEAR_FIRST:
            copies.send(
                ("back", d, position), summed.at[position, at_z(d)], back.at[position, g], to_z(d)
            )
        back[position, g] = summed[position, g]

    attend(0)
    for unit in out_units:
        unit_relay(*unit)
    over_y("wkv", wkv)
    receive_normed(1)
    attend(1)
    for unit in out_units:
        unit_far(*unit)
    for d in NEAR_FIRST:
        copies.wait(("wkv", "y", d), wkv.at[q, pl.ds(at_y(-d) * 4, 4)], to_y(d))
    for k in NEAR_FIRST:
        there = (x + k) % 4
        part = wkv.at[q, pl.ds(there * 4, 4)]
        copies.send(("wkv", "x", k), part, part, to_x(k))
    own_heads = pl.ds(x * 4, 4)
    copies.send(("wkv", "core", 0), wkv.at[q, own_heads], wkv.at[q, own_heads], sibling)
    for unit in out_units:
        unit_end(*unit[:3])
    project(0)
    project(1)

    for k in NEAR_FIRST:
        part = wkv.at[at_x(-k), own_heads]
        copies.wait(("wkv", "x", k), part, to_x(k))
        copies.send(("wkv", "core", k), part, part, sibling)
    copies.drain(early)
    copies.wait("start_after", start_in.at[0], after)
    copies.wait("start_before", start_in.at[1], before)

    pool_gain = pool_gain_ref[...]

    def pool_norm(position, number, source):
        value = layer_norm(back[position, source].astype(F32), pool_gain)
        pooled[x, position, source] = value.astype(BF16)
        part = pooled.at[x, position, source]
        for k in NEAR_FIRST:
            copies.send(("pooled", k, position, number), part, part, to_x(k))

    pool_norm(0, 0, g)
    pool_norm(1, 0, g)
    for d in (0,) + NEAR_FIRST:
        other = ((x - d + 4) % 4) * 2 + 1 - c
        copies.wait(("wkv", "core", d), wkv.at[other, own_heads], sibling)

    wide_lane = lax.broadcasted_iota(jnp.int32, (64, 256), 1)
    for head in range(4):
        parts = [wkv[2 * block, 4 * x + head, 128:144, :] for block in range(4)]
        query = jnp.concatenate(parts, axis=0)
        query = jnp.concatenate([query, query], axis=1)
        block_queries[head * 64 : head * 64 + 64, :] = jnp.where(
            (wide_lane >> 6) == head, query, jnp.zeros_like(query)
        )

    for position in range(2):
        for number, d in ((1, 1), (2, 3), (3, 2)):
            copies.wait(("back", d, position), back.at[position, at_z(-d)], to_z(d))
            pool_norm(position, number, at_z(-d))

    far_starts = jnp.where(lane < 64, start_in[1], start_in[0])[0:1]
    own_starts = start_out[0:1, :]
    frame = t * 16 + (lax.broadcasted_iota(jnp.int32, (128, 256), 0) & 15)
    in_lane = lax.broadcasted_iota(jnp.int32, (1, 128), 1)

    def live_of(starts, second):
        half = jnp.where((in_lane >= 64) == second, starts, -(10**6))
        start = jnp.max(half, axis=1, keepdims=True)
        return (frame >= start) & (frame < start + CLIP) & (frame < valid)

    live = [
        live_of(own_starts, False),
        live_of(own_starts, True),
        live_of(far_starts, False),
        live_of(far_starts, True),
    ]
    pair_lane = lax.broadcasted_iota(jnp.int32, (64, 128), 1)
    key_blocks, value_blocks = [], []
    for block in range(8):
        four = wkv[block, own_heads]
        key_blocks.append(four[:, 0:64, :].reshape(256, 128))
        value_blocks.append(four[:, 64:128, :].reshape(256, 128))
    key_weight = jnp.concatenate(key_blocks, axis=1)
    value_weight = jnp.concatenate(value_blocks, axis=1)

    def pool_project(place, source):
        here = pooled[source].reshape(128, D)
        key = dot_nt(here, key_weight).astype(BF16)
        scores_at[place] = dot(key, block_queries[...]) * SCALE
        values[:, place * 128 : place * 128 + 128] = dot_nt(value_weight, here).astype(BF16)

    pool_project(0, x)
    for place, k in ((1, 1), (2, 3), (3, 2)):
        source = (x - k + 4) % 4
        for position in range(2):
            for number, d in enumerate((0, 1, 3, 2)):
                part = pooled.at[source, position, at_z(-d)]
                copies.wait(("pooled", k, position, number), part, to_x(k))
        pool_project(place, source)

    for clip in range(4):
        top = jnp.full((1, 256), NEG, F32)
        for place in range(4):
            kept = jnp.where(live[clip], scores_at[place], NEG)
            top = jnp.maximum(top, jnp.max(kept, axis=0, keepdims=True))
        weights = [
            jnp.where(live[clip], jnp.exp(scores_at[place] - top), 0.0) for place in range(4)
        ]
        total = sum(jnp.sum(weight, axis=0, keepdims=True) for weight in weights)
        mix = dot(values[...], jnp.concatenate([w.astype(BF16) for w in weights], axis=0))
        for pair in range(2):
            cols = slice(pair * 128, pair * 128 + 128)
            even = mix[pair * 128 : pair * 128 + 64, cols]
            odd = mix[pair * 128 + 64 : pair * 128 + 128, cols]
            part_out[pair, clip * 64 : clip * 64 + 64, :] = jnp.where(
                pair_lane < 64, even, odd
            ).astype(BF16)
            stat_out[pair, clip : clip + 1, :] = top[:, cols]
            stat_out[pair, 4 + clip : 5 + clip, :] = total[:, cols]
    copies.send("part", part_out.at[1 - c], part_in, sibling)
    copies.send("stat", stat_out.at[1 - c], stat_in, sibling)

    key_blocks, value_blocks = [], []
    for block in range(8):
        two = wkv[block, pl.ds(q * 2, 2)]
        key_blocks.append(two[:, 0:64, :].reshape(128, 128))
        value_blocks.append(two[:, 64:128, :].reshape(128, 128))
    self_key = dot_nt(latn[...], jnp.concatenate(key_blocks, axis=1)).astype(BF16)
    self_value = dot_nt(jnp.concatenate(value_blocks, axis=1), latn[...]).astype(BF16)
    pair_queries = jnp.where(
        c == 0, block_queries[0:128, 0:128], block_queries[128:256, 128:256]
    )
    self_scores = dot(self_key, pair_queries) * SCALE
    self_top = jnp.max(self_scores, axis=0, keepdims=True)

    by_frame = jnp.where(
        from_row == (to_row & 1) * 64 + ((to_row & 7) >> 1) * 16 + (to_row >> 3), 1.0, 0.0
    ).astype(BF16)
    held = back[...].reshape(128, D)
    for half in range(2):
        cols = slice(half * 512, half * 512 + 512)
        temporal_ref[:, cols] = dot(by_frame, held[:, cols]).astype(BF16)

    copies.wait("part", part_in, sibling)
    copies.wait("stat", stat_in, sibling)
    stats = [stat_out[c], stat_in[...]]
    highest = stats[0][0:4]
    for stat in stats[1:]:
        highest = jnp.maximum(highest, stat[0:4])
    factors = [jnp.exp(stat[0:4] - highest) for stat in stats]
    totals = jnp.zeros((4, 128), F32)
    for stat, factor in zip(stats, factors):
        totals += stat[4:8] * factor
    nstat_out[0:4, :] = highest
    nstat_out[4:8, :] = totals

    def gathered(clip):
        mix = jnp.zeros((64, 128), F32)
        span = slice(clip * 64, clip * 64 + 64)
        for part, factor in zip((part_out[c, span, :], part_in[span, :]), factors):
            mix += part.astype(F32) * factor[clip : clip + 1]
        return mix

    near_out[0] = gathered(2).astype(BF16)
    copies.send("near_after", near_out.at[0], near_in.at[0], after)
    copies.send("nstat_after", nstat_out, nstat_in.at[0], after)
    near_out[1] = gathered(3).astype(BF16)
    copies.send("near_before", near_out.at[1], near_in.at[1], before)
    copies.send("nstat_before", nstat_out, nstat_in.at[1], before)
    own_mixes = [gathered(0), gathered(1)]

    finished = []
    for clip, name, device in ((0, "after", after), (1, "before", before)):
        copies.wait(f"near_{name}", near_in.at[clip], device)
        copies.wait(f"nstat_{name}", nstat_in.at[clip], device)
        near_top = nstat_in[clip, 2 + clip : 3 + clip, :]
        near_total = nstat_in[clip, 6 + clip : 7 + clip, :]
        own_top = highest[clip : clip + 1]
        top = jnp.maximum(jnp.maximum(own_top, near_top), self_top)
        own_factor = jnp.exp(own_top - top)
        near_factor = jnp.exp(near_top - top)
        weights = jnp.exp(self_scores - top)
        total = (
            totals[clip : clip + 1] * own_factor
            + near_total * near_factor
            + jnp.sum(weights, axis=0, keepdims=True)
        )
        self_mix = dot(self_value, weights.astype(BF16))
        self_mix = jnp.where(pair_lane < 64, self_mix[0:64], self_mix[64:128])
        mix = own_mixes[clip] * own_factor + near_in[clip].astype(F32) * near_factor + self_mix
        finished.append(mix / total)

    turned = jnp.transpose(jnp.concatenate(finished, axis=0))
    even, odd = turned[0:64], turned[64:128]
    piece_out[0:64, :] = jnp.where(pair_lane < 64, even, pltpu.roll(odd, 64, 1)).astype(BF16)
    piece_out[64:128, :] = jnp.where(pair_lane < 64, pltpu.roll(even, 64, 1), odd).astype(BF16)
    for d in range(1, 8):
        copies.send(("piece", d), piece_out, piece_in.at[q], to_patch(d))
    piece_in[q] = piece_out[...]
    for d in range(1, 8):
        copies.wait(("piece", d), piece_in.at[(q + 8 - d) % 8], to_patch(d))
    for block in range(8):
        pooled_ref[:, block * 128 : block * 128 + 128] = piece_in[block]
    copies.drain()
    assert len(copies.slots) <= SLOTS


def on_device(
    tokens,
    frame_gain,
    qkv_weight,
    out_weight,
    pool_gain,
    latent_gain,
    latents,
    query_weight,
    kv_weight,
    clip_starts,
    valid_frames,
):
    frames_dev, patch_dev, width = tokens.shape
    vmem = pl.BlockSpec(memory_space=pltpu.VMEM)
    temporal_out, pooled = pl.pallas_call(
        kernel,
        out_shape=(
            jax.ShapeDtypeStruct((128, D), BF16),
            jax.ShapeDtypeStruct((128, D), BF16),
        ),
        in_specs=[pl.BlockSpec(memory_space=pl.ANY)] * 11,
        out_specs=(vmem, vmem),
        scratch_shapes=[
            pltpu.SMEM((2,), jnp.int32),
            pltpu.SMEM((1,), jnp.int32),
            pltpu.VMEM((128, D), BF16),
            pltpu.VMEM((1, D), F32),
            pltpu.VMEM((1, D), F32),
            pltpu.VMEM((1, D), F32),
            pltpu.VMEM((64, D), BF16),
            pltpu.VMEM((64, D), BF16),
            pltpu.VMEM((128, 128), BF16),
            pltpu.VMEM((2, 4, 16, D), BF16),
            pltpu.VMEM((2, 4, 16, D), BF16),
            pltpu.VMEM((2, 16, 16, D), BF16),
            pltpu.VMEM((8, 4, 192, 128), BF16),
            pltpu.VMEM((8, 16, 64, 128), BF16),
            pltpu.VMEM((8, 16, 144, 128), BF16),
            pltpu.VMEM((2, 4, 64, 256), BF16),
            pltpu.VMEM((2, 4, 64, 256), BF16),
            pltpu.VMEM((2, 4, 16, D), BF16),
            pltpu.VMEM((2, 4, 16, D), BF16),
            pltpu.VMEM((4, 2, 4, 16, D), BF16),
            pltpu.VMEM((64, D), BF16),
            pltpu.VMEM((4, 16, 128), BF16),
            pltpu.VMEM((256, 256), BF16),
            pltpu.VMEM((4, 128, 256), F32),
            pltpu.VMEM((256, 512), BF16),
            pltpu.VMEM((8, 128), jnp.int32),
            pltpu.VMEM((2, 8, 128), jnp.int32),
            pltpu.VMEM((2, 256, 128), BF16),
            pltpu.VMEM((256, 128), BF16),
            pltpu.VMEM((2, 8, 128), F32),
            pltpu.VMEM((8, 128), F32),
            pltpu.VMEM((2, 64, 128), BF16),
            pltpu.VMEM((2, 64, 128), BF16),
            pltpu.VMEM((8, 128), F32),
            pltpu.VMEM((2, 8, 128), F32),
            pltpu.VMEM((128, 128), BF16),
            pltpu.VMEM((8, 128, 128), BF16),
            pltpu.SemaphoreType.DMA((18,)),
            pltpu.SemaphoreType.DMA((SLOTS,)),
            pltpu.SemaphoreType.DMA((SLOTS,)),
        ],
        compiler_params=pltpu.CompilerParams(
            collective_id=0, has_side_effects=True, vmem_limit_bytes=62 * 1024 * 1024
        ),
    )(
        clip_starts,
        valid_frames,
        tokens.reshape(frames_dev * patch_dev, width),
        frame_gain.reshape(1, width),
        qkv_weight.T,
        out_weight,
        pool_gain.reshape(1, width),
        latent_gain.reshape(1, width),
        latents,
        query_weight.T,
        kv_weight,
    )
    return (
        temporal_out.reshape(frames_dev, patch_dev, width),
        pooled.reshape(2, 64, width),
    )


def solution(mesh):
    in_specs = (
        P(("dp", "tm"), "patch", None),
        P(),
        P(None, "tm"),
        P("tm", None),
        P(),
        P(),
        P(),
        P(None, "tm"),
        P(None, "tm"),
        P(("dp", "tm")),
        P("dp"),
    )
    out_specs = (P(("dp", "tm"), "patch", None), P(("dp", "tm"), None, None))
    return jax.shard_map(
        on_device, mesh=mesh, in_specs=in_specs, out_specs=out_specs, check_vma=False
    )
```

```python
import jax
import jax.numpy as jnp
from jax import lax
from jax.experimental import pallas as pl
from jax.experimental.pallas import tpu as pltpu
from jax.sharding import PartitionSpec as P

MESH = pl.DeviceIdType.MESH
F32 = jnp.float32
BF16 = jnp.bfloat16
D = 1024
HEAD = 64
CLIP = 16
EPS = 1e-05
NEG = -1e30
SCALE = HEAD ** (-0.5)
SLOTS = 144
NEAR_FIRST = (1, 3, 2)


def layer_norm(value, gain):
    center = value - jnp.mean(value, axis=-1, keepdims=True)
    spread = jnp.mean(center * center, axis=-1, keepdims=True)
    return center * lax.rsqrt(spread + EPS) * gain


def dot(a, b):
    return jnp.dot(a, b, preferred_element_type=F32)


def dot_nt(a, b):
    return lax.dot_general(a, b, (((1,), (1,)), ((), ())), preferred_element_type=F32)


class Copies:
    def __init__(self, send_sem, recv_sem):
        self.send_sem = send_sem
        self.recv_sem = recv_sem
        self.slots = {}
        self.started = []

    def slot(self, name):
        return self.slots.setdefault(name, len(self.slots))

    def make(self, name, src, dst, device):
        slot = self.slot(name)
        return pltpu.make_async_remote_copy(
            src_ref=src,
            dst_ref=dst,
            send_sem=self.send_sem.at[slot],
            recv_sem=self.recv_sem.at[slot],
            device_id=device,
            device_id_type=MESH,
        )

    def send(self, name, src, dst, device):
        copy = self.make(name, src, dst, device)
        copy.start()
        self.started.append(copy)

    def wait(self, name, dst, device):
        self.make(name, dst, dst, device).wait_recv()

    def drain(self, count=None):
        done, self.started = self.started[:count], self.started[len(self.started[:count]) :]
        for copy in done:
            copy.wait_send()


def kernel(
    starts_hbm,
    valid_hbm,
    tokens_hbm,
    frame_gain_hbm,
    qkv_hbm,
    out_w_hbm,
    pool_gain_hbm,
    latent_gain_hbm,
    latents_hbm,
    query_w_hbm,
    kv_w_hbm,
    temporal_ref,
    pooled_ref,
    starts_ref,
    valid_ref,
    tokens_ref,
    frame_gain_ref,
    pool_gain_ref,
    latent_gain_ref,
    latents_ref,
    query_w_ref,
    kv_w_ref,
    own_rows,
    rows,
    normed,
    wqkv,
    wout,
    wkv,
    att_out,
    att_in,
    summed,
    back,
    pooled,
    latn,
    held_queries,
    block_queries,
    scores_at,
    values,
    start_out,
    start_in,
    part_out,
    part_in,
    stat_out,
    stat_in,
    near_out,
    near_in,
    nstat_out,
    nstat_in,
    piece_out,
    piece_in,
    load_sem,
    send_sem,
    recv_sem,
):
    t = lax.axis_index("tm")
    q = lax.axis_index("patch")
    y, g = t // 4, t % 4
    x, c = q // 2, q % 2
    copies = Copies(send_sem, recv_sem)

    def at_z(d):
        return (g + d + 4) % 4

    def at_y(d):
        return (y + d + 4) % 4

    def at_x(d):
        return ((x + d + 4) % 4) * 2 + c

    def to_z(d):
        return {"tm": y * 4 + at_z(d)}

    def to_y(d):
        return {"tm": at_y(d) * 4 + g}

    def to_x(d):
        return {"patch": at_x(d)}

    def to_patch(d):
        return {"patch": (q + d) % 8}

    sibling = {"patch": x * 2 + 1 - c}
    after = {"tm": (t + 1) % 16}
    before = {"tm": (t + 15) % 16}

    eighth = pl.ds(pl.multiple_of(q * 128, 128), 128)
    loads = [
        pltpu.make_async_copy(src, dst, load_sem.at[number])
        for number, (src, dst) in enumerate(
            [(tokens_hbm, tokens_ref)]
            + [(qkv_hbm.at[:, pl.ds(b * 128, 128)], wqkv.at[b, 0]) for b in range(8)]
            + [
                (out_w_hbm.at[:, eighth], wout.at[q, 0, 0]),
                (frame_gain_hbm, frame_gain_ref),
                (latents_hbm, latents_ref),
                (latent_gain_hbm, latent_gain_ref),
                (query_w_hbm, query_w_ref),
                (kv_w_hbm.at[eighth, :], kv_w_ref),
                (pool_gain_hbm, pool_gain_ref),
                (starts_hbm, starts_ref),
                (valid_hbm, valid_ref),
            ]
        )
    ]
    for load in loads:
        load.start()

    barrier = pltpu.get_barrier_semaphore()
    partners = (
        [to_z(d) for d in (1, 2, 3)]
        + [to_y(d) for d in (1, 2, 3)]
        + [to_patch(d) for d in range(1, 8)]
        + [after, before]
    )
    for partner in partners:
        pl.semaphore_signal(barrier, inc=1, device_id=partner, device_id_type=MESH)

    to_row = lax.broadcasted_iota(jnp.int32, (128, 128), 0)
    from_row = lax.broadcasted_iota(jnp.int32, (128, 128), 1)
    by_position = jnp.where(
        from_row == (to_row & 15) * 8 + ((to_row >> 4) & 3) * 2 + (to_row >> 6), 1.0, 0.0
    ).astype(BF16)
    loads[0].wait()
    for half in range(2):
        cols = slice(half * 512, half * 512 + 512)
        moved = dot(by_position, tokens_ref[:, cols]).astype(BF16)
        own_rows[:, :, :, cols] = moved.reshape(2, 4, 16, 512)
    for load in loads[1:10]:
        load.wait()

    pl.semaphore_wait(barrier, len(partners))

    for d in NEAR_FIRST:
        copies.send(f"wqkv_z{d}", wqkv.at[q, 0], wqkv.at[q, d], to_z(d))
    for d in NEAR_FIRST:
        copies.send(f"wout_z{d}", wout.at[q, 0, 0], wout.at[q, 0, d], to_z(d))
    def send_rows(position):
        for d in NEAR_FIRST:
            copies.send(
                ("rows", d, position),
                own_rows.at[position, at_z(d)],
                rows.at[position, g],
                to_z(d),
            )

    send_rows(0)
    send_rows(1)

    for load in loads[10:]:
        load.wait()
    lane = lax.broadcasted_iota(jnp.int32, (8, 128), 1)
    start_out[...] = jnp.where(lane < 64, starts_ref[0], starts_ref[1])
    copies.send("start_after", start_out, start_in.at[0], after)
    copies.send("start_before", start_out, start_in.at[1], before)

    frame_gain = frame_gain_ref[...]

    def spread_rows(position, number, source):
        shard = y * 4 + source
        value = layer_norm(rows[position, source].astype(F32), frame_gain)
        normed[position, shard] = value.astype(BF16)
        part = normed.at[position, shard]
        for d in NEAR_FIRST:
            copies.send(("normed", d, position, number), part, part, to_y(d))

    def receive_rows(position):
        for number, d in ((1, 1), (2, 3), (3, 2)):
            copies.wait(("rows", d, position), rows.at[position, at_z(-d)], to_z(d))
            spread_rows(position, number, at_z(-d))

    def receive_normed(position):
        for number, source in enumerate((0, 1, 3, 2)):
            for d in NEAR_FIRST:
                shard = at_y(-d) * 4 + at_z(-source)
                copies.wait(("normed", d, position, number), normed.at[position, shard], to_y(d))

    for position in range(2):
        rows[position, g] = own_rows[position, g]
        spread_rows(position, 0, g)

    latn[...] = layer_norm(latents_ref[...].astype(F32), latent_gain_ref[...]).astype(BF16)
    queries = dot_nt(query_w_ref[...], latn[...])
    held_queries[...] = jnp.concatenate([queries, queries], axis=1).astype(BF16).reshape(4, 16, 128)
    wkv[q, t, 0:128, :] = jnp.transpose(kv_w_ref[...].astype(F32)).astype(BF16)
    wkv[q, t, 128:144, :] = held_queries[q // 2]

    def unit_start(name, buf, part):
        copies.send((name, "right"), part(buf, q), part(buf, q), to_x(1))
        copies.send((name, "left"), part(buf, q), part(buf, q), to_x(-1))
        copies.send((name, "core", 0), part(buf, q), part(buf, q), sibling)

    def unit_relay(name, buf, part, low, high):
        copies.wait((name, "right"), part(buf, at_x(-1)), to_x(1))
        copies.send((name, "relay_right"), low(buf, at_x(-1)), low(buf, at_x(-1)), to_x(1))
        copies.send((name, "core", 1), part(buf, at_x(-1)), part(buf, at_x(-1)), sibling)
        copies.wait((name, "left"), part(buf, at_x(1)), to_x(-1))
        copies.send((name, "relay_left"), high(buf, at_x(1)), high(buf, at_x(1)), to_x(-1))
        copies.send((name, "core", 2), part(buf, at_x(1)), part(buf, at_x(1)), sibling)

    def unit_far(name, buf, part, low, high):
        copies.wait((name, "relay_right"), low(buf, at_x(2)), to_x(1))
        copies.wait((name, "relay_left"), high(buf, at_x(2)), to_x(-1))
        copies.send((name, "core", 3), part(buf, at_x(2)), part(buf, at_x(2)), sibling)

    def unit_end(name, buf, part):
        for number, d in enumerate((0, -1, 1, 2)):
            other = ((x + d + 4) % 4) * 2 + 1 - c
            copies.wait((name, "core", number), part(buf, other), sibling)

    qkv_unit = (
        "wqkv",
        wqkv,
        lambda buf, at: buf.at[at, pl.ds(1, 3)],
        lambda buf, at: buf.at[at, pl.ds(1, 3), pl.ds(0, 96)],
        lambda buf, at: buf.at[at, pl.ds(1, 3), pl.ds(96, 96)],
    )
    out_unit = (
        "wout",
        wout,
        lambda buf, at: buf.at[at],
        lambda buf, at: buf.at[at, pl.ds(0, 2)],
        lambda buf, at: buf.at[at, pl.ds(2, 2)],
    )

    for d in NEAR_FIRST:
        copies.wait(f"wqkv_z{d}", wqkv.at[q, d], to_z(d))
    unit_start(*qkv_unit[:3])
    for d in NEAR_FIRST:
        copies.wait(f"wout_z{d}", wout.at[q, 0, d], to_z(d))
    for d in NEAR_FIRST:
        copies.send(f"wout_y{d}", wout.at[q, 0], wout.at[q, d], to_y(d))
    receive_rows(0)
    unit_relay(*qkv_unit)
    for d in NEAR_FIRST:
        copies.send(f"wkv_z{d}", wkv.at[q, t], wkv.at[q, t], to_z(d))
    for d in NEAR_FIRST:
        copies.wait(f"wout_y{d}", wout.at[q, d], to_y(d))
    unit_start(*out_unit[:3])
    receive_rows(1)
    unit_far(*qkv_unit)
    receive_normed(0)
    unit_end(*qkv_unit[:3])
    early = len(copies.started)

    valid = valid_ref[0]
    key_live = lax.broadcasted_iota(jnp.int32, (256, 256), 1) < valid
    first_head = lax.broadcasted_iota(jnp.int32, (256, 128), 1) < 64

    def attend(position):
        here = normed[position].reshape(256, D)
        for pair in range(2):
            blocks = []
            for block in range(8):
                parts = [
                    wqkv[block, 2 * pair + head, kind * 64 : kind * 64 + 64, :]
                    for kind in range(3)
                    for head in range(2)
                ]
                blocks.append(jnp.concatenate(parts, axis=0))
            weight = jnp.concatenate(blocks, axis=1)
            projected = dot_nt(here, weight).astype(BF16)
            query, key, value = (projected[:, k * 128 : k * 128 + 128] for k in range(3))
            mixed = []
            for head in range(2):
                mine = first_head if head == 0 else jnp.logical_not(first_head)
                scores = dot_nt(jnp.where(mine, query, jnp.zeros_like(query)), key) * SCALE
                scores = jnp.where(key_live, scores, -jnp.inf)
                weights = jnp.exp(scores - jnp.max(scores, axis=-1, keepdims=True))
                total = jnp.sum(weights, axis=-1, keepdims=True)
                mixed.append(dot(weights.astype(BF16), value) / total)
            result = jnp.where(first_head, mixed[0], mixed[1]).astype(BF16)
            att_out[position, :, :, pair * 128 : pair * 128 + 128] = result.reshape(4, 64, 128)
        for d in NEAR_FIRST:
            copies.send(
                ("att", d, position), att_out.at[position, at_y(d)], att_in.at[position, d], to_y(d)
            )
        att_in[position, 0] = att_out[position, y]

    def project(position):
        for d in NEAR_FIRST:
            copies.wait(("att", d, position), att_in.at[position, d], to_y(d))
        attended = jnp.concatenate([att_in[position, source] for source in range(4)], axis=1)
        for block in range(4):
            weight = jnp.concatenate(
                [wout[2 * block].reshape(D, 128), wout[2 * block + 1].reshape(D, 128)], axis=1
            )
            cols = slice(block * 256, block * 256 + 256)
            tokens = rows[position, :, :, cols]
            total = tokens.astype(F32).reshape(64, 256) + dot(attended, weight)
            summed[position, :, :, cols] = total.astype(BF16).reshape(4, 16, 256)
        for d in NEAR_FIRST:
            copies.send(
                ("back", d, position), summed.at[position, at_z(d)], back.at[position, g], to_z(d)
            )
        back[position, g] = summed[position, g]

    attend(0)
    unit_relay(*out_unit)
    for d in NEAR_FIRST:
        copies.wait(f"wkv_z{d}", wkv.at[q, y * 4 + at_z(-d)], to_z(d))
    part = wkv.at[q, pl.ds(y * 4, 4)]
    for d in NEAR_FIRST:
        copies.send(("wkv", "y", d), part, part, to_y(d))
    receive_normed(1)
    attend(1)
    unit_far(*out_unit)
    for d in NEAR_FIRST:
        copies.wait(("wkv", "y", d), wkv.at[q, pl.ds(at_y(-d) * 4, 4)], to_y(d))
    for k in NEAR_FIRST:
        there = (x + k) % 4
        part = wkv.at[q, pl.ds(there * 4, 4)]
        copies.send(("wkv", "x", k), part, part, to_x(k))
    own_heads = pl.ds(x * 4, 4)
    copies.send(("wkv", "core", 0), wkv.at[q, own_heads], wkv.at[q, own_heads], sibling)
    unit_end(*out_unit[:3])
    project(0)
    project(1)

    for k in NEAR_FIRST:
        part = wkv.at[at_x(-k), own_heads]
        copies.wait(("wkv", "x", k), part, to_x(k))
        copies.send(("wkv", "core", k), part, part, sibling)
    copies.drain(early)
    copies.wait("start_after", start_in.at[0], after)
    copies.wait("start_before", start_in.at[1], before)

    pool_gain = pool_gain_ref[...]

    def pool_norm(position, number, source):
        value = layer_norm(back[position, source].astype(F32), pool_gain)
        pooled[x, position, source] = value.astype(BF16)
        part = pooled.at[x, position, source]
        for k in NEAR_FIRST:
            copies.send(("pooled", k, position, number), part, part, to_x(k))

    def receive_back(position):
        for number, d in ((1, 1), (2, 3), (3, 2)):
            copies.wait(("back", d, position), back.at[position, at_z(-d)], to_z(d))
            pool_norm(position, number, at_z(-d))

    pool_norm(0, 0, g)
    pool_norm(1, 0, g)
    for d in (0,) + NEAR_FIRST:
        other = ((x - d + 4) % 4) * 2 + 1 - c
        copies.wait(("wkv", "core", d), wkv.at[other, own_heads], sibling)

    wide_lane = lax.broadcasted_iota(jnp.int32, (64, 256), 1)
    for head in range(4):
        parts = [wkv[2 * block, 4 * x + head, 128:144, :] for block in range(4)]
        query = jnp.concatenate(parts, axis=0)
        query = jnp.concatenate([query, query], axis=1)
        block_queries[head * 64 : head * 64 + 64, :] = jnp.where(
            (wide_lane >> 6) == head, query, jnp.zeros_like(query)
        )

    key_blocks, value_blocks = [], []
    for block in range(8):
        two = wkv[block, pl.ds(q * 2, 2)]
        key_blocks.append(two[:, 0:64, :].reshape(128, 128))
        value_blocks.append(two[:, 64:128, :].reshape(128, 128))
    self_key = dot_nt(latn[...], jnp.concatenate(key_blocks, axis=1)).astype(BF16)
    self_value = dot_nt(jnp.concatenate(value_blocks, axis=1), latn[...]).astype(BF16)
    pair_queries = jnp.where(
        c == 0, block_queries[0:128, 0:128], block_queries[128:256, 128:256]
    )
    self_scores = dot(self_key, pair_queries) * SCALE
    self_top = jnp.max(self_scores, axis=0, keepdims=True)

    for position in range(2):
        receive_back(position)

    far_starts = jnp.where(lane < 64, start_in[1], start_in[0])[0:1]
    own_starts = start_out[0:1, :]
    frame = t * 16 + (lax.broadcasted_iota(jnp.int32, (128, 256), 0) & 15)
    in_lane = lax.broadcasted_iota(jnp.int32, (1, 128), 1)

    def live_of(starts, second):
        half = jnp.where((in_lane >= 64) == second, starts, -(10**6))
        start = jnp.max(half, axis=1, keepdims=True)
        return (frame >= start) & (frame < start + CLIP) & (frame < valid)

    live = [
        live_of(own_starts, False),
        live_of(own_starts, True),
        live_of(far_starts, False),
        live_of(far_starts, True),
    ]
    pair_lane = lax.broadcasted_iota(jnp.int32, (64, 128), 1)
    key_blocks, value_blocks = [], []
    for block in range(8):
        four = wkv[block, own_heads]
        key_blocks.append(four[:, 0:64, :].reshape(256, 128))
        value_blocks.append(four[:, 64:128, :].reshape(256, 128))
    key_weight = jnp.concatenate(key_blocks, axis=1)
    value_weight = jnp.concatenate(value_blocks, axis=1)

    def pool_project(place, source):
        here = pooled[source].reshape(128, D)
        key = dot_nt(here, key_weight).astype(BF16)
        scores_at[place] = dot(key, block_queries[...]) * SCALE
        values[:, place * 128 : place * 128 + 128] = dot_nt(value_weight, here).astype(BF16)

    pool_project(0, x)

    by_frame = jnp.where(
        from_row == (to_row & 1) * 64 + ((to_row & 7) >> 1) * 16 + (to_row >> 3), 1.0, 0.0
    ).astype(BF16)
    held = back[...].reshape(128, D)
    for half in range(2):
        cols = slice(half * 512, half * 512 + 512)
        temporal_ref[:, cols] = dot(by_frame, held[:, cols]).astype(BF16)
    for place, k in ((1, 1), (2, 3), (3, 2)):
        source = (x - k + 4) % 4
        for position in range(2):
            for number, d in enumerate((0, 1, 3, 2)):
                part = pooled.at[source, position, at_z(-d)]
                copies.wait(("pooled", k, position, number), part, to_x(k))
        pool_project(place, source)

    for clip in range(4):
        top = jnp.full((1, 256), NEG, F32)
        for place in range(4):
            kept = jnp.where(live[clip], scores_at[place], NEG)
            top = jnp.maximum(top, jnp.max(kept, axis=0, keepdims=True))
        weights = [
            jnp.where(live[clip], jnp.exp(scores_at[place] - top), 0.0) for place in range(4)
        ]
        total = sum(jnp.sum(weight, axis=0, keepdims=True) for weight in weights)
        mix = dot(values[...], jnp.concatenate([w.astype(BF16) for w in weights], axis=0))
        for pair in range(2):
            cols = slice(pair * 128, pair * 128 + 128)
            even = mix[pair * 128 : pair * 128 + 64, cols]
            odd = mix[pair * 128 + 64 : pair * 128 + 128, cols]
            part_out[pair, clip * 64 : clip * 64 + 64, :] = jnp.where(
                pair_lane < 64, even, odd
            ).astype(BF16)
            stat_out[pair, clip : clip + 1, :] = top[:, cols]
            stat_out[pair, 4 + clip : 5 + clip, :] = total[:, cols]
    copies.send("part", part_out.at[1 - c], part_in, sibling)
    copies.send("stat", stat_out.at[1 - c], stat_in, sibling)

    copies.wait("part", part_in, sibling)
    copies.wait("stat", stat_in, sibling)
    stats = [stat_out[c], stat_in[...]]
    highest = stats[0][0:4]
    for stat in stats[1:]:
        highest = jnp.maximum(highest, stat[0:4])
    factors = [jnp.exp(stat[0:4] - highest) for stat in stats]
    totals = jnp.zeros((4, 128), F32)
    for stat, factor in zip(stats, factors):
        totals += stat[4:8] * factor
    nstat_out[0:4, :] = highest
    nstat_out[4:8, :] = totals

    def gathered(clip):
        mix = jnp.zeros((64, 128), F32)
        span = slice(clip * 64, clip * 64 + 64)
        for part, factor in zip((part_out[c, span, :], part_in[span, :]), factors):
            mix += part.astype(F32) * factor[clip : clip + 1]
        return mix

    near_out[0] = gathered(2).astype(BF16)
    copies.send("near_after", near_out.at[0], near_in.at[0], after)
    copies.send("nstat_after", nstat_out, nstat_in.at[0], after)
    near_out[1] = gathered(3).astype(BF16)
    copies.send("near_before", near_out.at[1], near_in.at[1], before)
    copies.send("nstat_before", nstat_out, nstat_in.at[1], before)
    own_mixes = [gathered(0), gathered(1)]

    finished = []
    for clip, name, device in ((0, "after", after), (1, "before", before)):
        copies.wait(f"near_{name}", near_in.at[clip], device)
        copies.wait(f"nstat_{name}", nstat_in.at[clip], device)
        near_top = nstat_in[clip, 2 + clip : 3 + clip, :]
        near_total = nstat_in[clip, 6 + clip : 7 + clip, :]
        own_top = highest[clip : clip + 1]
        top = jnp.maximum(jnp.maximum(own_top, near_top), self_top)
        own_factor = jnp.exp(own_top - top)
        near_factor = jnp.exp(near_top - top)
        weights = jnp.exp(self_scores - top)
        total = (
            totals[clip : clip + 1] * own_factor
            + near_total * near_factor
            + jnp.sum(weights, axis=0, keepdims=True)
        )
        self_mix = dot(self_value, weights.astype(BF16))
        self_mix = jnp.where(pair_lane < 64, self_mix[0:64], self_mix[64:128])
        mix = own_mixes[clip] * own_factor + near_in[clip].astype(F32) * near_factor + self_mix
        finished.append(mix / total)

    turned = jnp.transpose(jnp.concatenate(finished, axis=0))
    even, odd = turned[0:64], turned[64:128]
    piece_out[0:64, :] = jnp.where(pair_lane < 64, even, pltpu.roll(odd, 64, 1)).astype(BF16)
    piece_out[64:128, :] = jnp.where(pair_lane < 64, pltpu.roll(even, 64, 1), odd).astype(BF16)
    for d in range(1, 8):
        copies.send(("piece", d), piece_out, piece_in.at[q], to_patch(d))
    piece_in[q] = piece_out[...]
    for d in range(1, 8):
        copies.wait(("piece", d), piece_in.at[(q + 8 - d) % 8], to_patch(d))
    for block in range(8):
        pooled_ref[:, block * 128 : block * 128 + 128] = piece_in[block]
    copies.drain()
    assert len(copies.slots) <= SLOTS


def on_device(
    tokens,
    frame_gain,
    qkv_weight,
    out_weight,
    pool_gain,
    latent_gain,
    latents,
    query_weight,
    kv_weight,
    clip_starts,
    valid_frames,
):
    frames_dev, patch_dev, width = tokens.shape
    vmem = pl.BlockSpec(memory_space=pltpu.VMEM)
    temporal_out, pooled = pl.pallas_call(
        kernel,
        out_shape=(
            jax.ShapeDtypeStruct((128, D), BF16),
            jax.ShapeDtypeStruct((128, D), BF16),
        ),
        in_specs=[pl.BlockSpec(memory_space=pl.ANY)] * 11,
        out_specs=(vmem, vmem),
        scratch_shapes=[
            pltpu.SMEM((2,), jnp.int32),
            pltpu.SMEM((1,), jnp.int32),
            pltpu.VMEM((128, D), BF16),
            pltpu.VMEM((1, D), F32),
            pltpu.VMEM((1, D), F32),
            pltpu.VMEM((1, D), F32),
            pltpu.VMEM((64, D), BF16),
            pltpu.VMEM((64, D), BF16),
            pltpu.VMEM((128, 128), BF16),
            pltpu.VMEM((2, 4, 16, D), BF16),
            pltpu.VMEM((2, 4, 16, D), BF16),
            pltpu.VMEM((2, 16, 16, D), BF16),
            pltpu.VMEM((8, 4, 192, 128), BF16),
            pltpu.VMEM((8, 4, 4, 64, 128), BF16),
            pltpu.VMEM((8, 16, 144, 128), BF16),
            pltpu.VMEM((2, 4, 64, 256), BF16),
            pltpu.VMEM((2, 4, 64, 256), BF16),
            pltpu.VMEM((2, 4, 16, D), BF16),
            pltpu.VMEM((2, 4, 16, D), BF16),
            pltpu.VMEM((4, 2, 4, 16, D), BF16),
            pltpu.VMEM((64, D), BF16),
            pltpu.VMEM((4, 16, 128), BF16),
            pltpu.VMEM((256, 256), BF16),
            pltpu.VMEM((4, 128, 256), F32),
            pltpu.VMEM((256, 512), BF16),
            pltpu.VMEM((8, 128), jnp.int32),
            pltpu.VMEM((2, 8, 128), jnp.int32),
            pltpu.VMEM((2, 256, 128), BF16),
            pltpu.VMEM((256, 128), BF16),
            pltpu.VMEM((2, 8, 128), F32),
            pltpu.VMEM((8, 128), F32),
            pltpu.VMEM((2, 64, 128), BF16),
            pltpu.VMEM((2, 64, 128), BF16),
            pltpu.VMEM((8, 128), F32),
            pltpu.VMEM((2, 8, 128), F32),
            pltpu.VMEM((128, 128), BF16),
            pltpu.VMEM((8, 128, 128), BF16),
            pltpu.SemaphoreType.DMA((18,)),
            pltpu.SemaphoreType.DMA((SLOTS,)),
            pltpu.SemaphoreType.DMA((SLOTS,)),
        ],
        compiler_params=pltpu.CompilerParams(
            collective_id=0, has_side_effects=True, vmem_limit_bytes=62 * 1024 * 1024
        ),
    )(
        clip_starts,
        valid_frames,
        tokens.reshape(frames_dev * patch_dev, width),
        frame_gain.reshape(1, width),
        qkv_weight.T,
        out_weight,
        pool_gain.reshape(1, width),
        latent_gain.reshape(1, width),
        latents,
        query_weight.T,
        kv_weight,
    )
    return (
        temporal_out.reshape(frames_dev, patch_dev, width),
        pooled.reshape(2, 64, width),
    )


def solution(mesh):
    in_specs = (
        P(("dp", "tm"), "patch", None),
        P(),
        P(None, "tm"),
        P("tm", None),
        P(),
        P(),
        P(),
        P(None, "tm"),
        P(None, "tm"),
        P(("dp", "tm")),
        P("dp"),
    )
    out_specs = (P(("dp", "tm"), "patch", None), P(("dp", "tm"), None, None))
    return jax.shard_map(
        on_device, mesh=mesh, in_specs=in_specs, out_specs=out_specs, check_vma=False
    )
```

```python
import jax
import jax.numpy as jnp
from jax import lax
from jax.experimental import pallas as pl
from jax.experimental.pallas import tpu as pltpu
from jax.sharding import PartitionSpec as P

MESH = pl.DeviceIdType.MESH
F32 = jnp.float32
BF16 = jnp.bfloat16
D = 1024
HEAD = 64
CLIP = 16
EPS = 1e-05
NEG = -1e30
SCALE = HEAD ** (-0.5)
SLOTS = 176
NEAR_FIRST = (1, 3, 2)


def layer_norm(value, gain):
    center = value - jnp.mean(value, axis=-1, keepdims=True)
    spread = jnp.mean(center * center, axis=-1, keepdims=True)
    return center * lax.rsqrt(spread + EPS) * gain


def dot(a, b):
    return jnp.dot(a, b, preferred_element_type=F32)


def dot_nt(a, b):
    return lax.dot_general(a, b, (((1,), (1,)), ((), ())), preferred_element_type=F32)


class Copies:
    def __init__(self, send_sem, recv_sem):
        self.send_sem = send_sem
        self.recv_sem = recv_sem
        self.slots = {}
        self.started = []

    def slot(self, name):
        return self.slots.setdefault(name, len(self.slots))

    def make(self, name, src, dst, device):
        slot = self.slot(name)
        return pltpu.make_async_remote_copy(
            src_ref=src,
            dst_ref=dst,
            send_sem=self.send_sem.at[slot],
            recv_sem=self.recv_sem.at[slot],
            device_id=device,
            device_id_type=MESH,
        )

    def send(self, name, src, dst, device):
        copy = self.make(name, src, dst, device)
        copy.start()
        self.started.append(copy)

    def wait(self, name, dst, device):
        self.make(name, dst, dst, device).wait_recv()

    def drain(self, count=None):
        done, self.started = self.started[:count], self.started[len(self.started[:count]) :]
        for copy in done:
            copy.wait_send()


def kernel(
    starts_hbm,
    valid_hbm,
    tokens_hbm,
    frame_gain_hbm,
    qkv_hbm,
    out_w_hbm,
    pool_gain_hbm,
    latent_gain_hbm,
    latents_hbm,
    query_w_hbm,
    kv_w_hbm,
    temporal_ref,
    pooled_ref,
    starts_ref,
    valid_ref,
    tokens_ref,
    frame_gain_ref,
    pool_gain_ref,
    latent_gain_ref,
    latents_ref,
    query_w_ref,
    kv_w_ref,
    own_rows,
    rows,
    normed,
    wqkv,
    wout,
    wkv,
    att_out,
    att_in,
    summed,
    back,
    pooled,
    latn,
    held_queries,
    block_queries,
    scores_at,
    values,
    start_out,
    start_in,
    part_out,
    part_in,
    stat_out,
    stat_in,
    near_out,
    near_in,
    nstat_out,
    nstat_in,
    piece_out,
    piece_in,
    load_sem,
    send_sem,
    recv_sem,
):
    t = lax.axis_index("tm")
    q = lax.axis_index("patch")
    y, g = t // 4, t % 4
    part_at = lax.axis_index("dp")
    x, c = q // 2, q % 2
    copies = Copies(send_sem, recv_sem)

    def at_z(d):
        return (g + d + 4) % 4

    def at_y(d):
        return (y + d + 4) % 4

    def at_x(d):
        return ((x + d + 4) % 4) * 2 + c

    def to_z(d):
        return {"tm": y * 4 + at_z(d)}

    def to_y(d):
        return {"tm": at_y(d) * 4 + g}

    def to_x(d):
        return {"patch": at_x(d)}

    def to_patch(d):
        return {"patch": (q + d) % 8}

    def to_dp(m):
        return {"dp": (part_at + m) % 4}

    sibling = {"patch": x * 2 + 1 - c}
    after = {"tm": (t + 1) % 16}
    before = {"tm": (t + 15) % 16}

    eighth = pl.ds(pl.multiple_of(q * 128, 128), 128)
    loads = [
        pltpu.make_async_copy(src, dst, load_sem.at[number])
        for number, (src, dst) in enumerate(
            [(tokens_hbm, tokens_ref)]
            + [(qkv_hbm.at[:, pl.ds(b * 128, 128)], wqkv.at[b, 0]) for b in range(8)]
            + [
                (out_w_hbm.at[:, eighth], wout.at[q, 0, 0]),
                (frame_gain_hbm, frame_gain_ref),
                (latents_hbm, latents_ref),
                (latent_gain_hbm, latent_gain_ref),
                (query_w_hbm, query_w_ref),
                (kv_w_hbm.at[eighth, :], kv_w_ref),
                (pool_gain_hbm, pool_gain_ref),
                (starts_hbm, starts_ref),
                (valid_hbm, valid_ref),
            ]
        )
    ]
    for load in loads:
        load.start()

    barrier = pltpu.get_barrier_semaphore()
    partners = (
        [to_z(d) for d in (1, 2, 3)]
        + [to_y(d) for d in (1, 2, 3)]
        + [to_patch(d) for d in range(1, 8)]
        + [after, before]
        + [to_dp(m) for m in (1, 2, 3)]
    )
    for partner in partners:
        pl.semaphore_signal(barrier, inc=1, device_id=partner, device_id_type=MESH)

    to_row = lax.broadcasted_iota(jnp.int32, (128, 128), 0)
    from_row = lax.broadcasted_iota(jnp.int32, (128, 128), 1)
    by_position = jnp.where(
        from_row == (to_row & 15) * 8 + ((to_row >> 4) & 3) * 2 + (to_row >> 6), 1.0, 0.0
    ).astype(BF16)
    loads[0].wait()
    for half in range(2):
        cols = slice(half * 512, half * 512 + 512)
        moved = dot(by_position, tokens_ref[:, cols]).astype(BF16)
        own_rows[:, :, :, cols] = moved.reshape(2, 4, 16, 512)
    for load in loads[1:10]:
        load.wait()

    pl.semaphore_wait(barrier, len(partners))

    def qkv_quarter(d, of):
        return wqkv.at[q, d, pl.ds(pl.multiple_of(of * 48, 16), 48)]

    def out_quarter(d, of):
        return wout.at[q, 0, d, pl.ds(pl.multiple_of(of * 16, 16), 16)]

    def quarter_z(name, quarter):
        for d in NEAR_FIRST:
            copies.send((name, "z", d), quarter(0, part_at), quarter(d, part_at), to_z(d))

    def quarter_dp(name, quarter):
        for d in NEAR_FIRST:
            copies.wait((name, "z", d), quarter(d, part_at), to_z(d))
            for m in (1, 3, 2):
                copies.send(
                    (name, "dp", d, m), quarter(d, part_at), quarter(d, part_at), to_dp(m)
                )

    def quarter_end(name, quarter):
        for d in NEAR_FIRST:
            for m in (1, 3, 2):
                copies.wait((name, "dp", d, m), quarter(d, (part_at + 4 - m) % 4), to_dp(m))

    quarter_z("wqkv", qkv_quarter)
    quarter_z("wout", out_quarter)
    def send_rows(position):
        for d in NEAR_FIRST:
            copies.send(
                ("rows", d, position),
                own_rows.at[position, at_z(d)],
                rows.at[position, g],
                to_z(d),
            )

    send_rows(0)
    send_rows(1)

    for load in loads[10:]:
        load.wait()
    lane = lax.broadcasted_iota(jnp.int32, (8, 128), 1)
    start_out[...] = jnp.where(lane < 64, starts_ref[0], starts_ref[1])
    copies.send("start_after", start_out, start_in.at[0], after)
    copies.send("start_before", start_out, start_in.at[1], before)

    frame_gain = frame_gain_ref[...]

    def spread_rows(position, number, source):
        shard = y * 4 + source
        value = layer_norm(rows[position, source].astype(F32), frame_gain)
        normed[position, shard] = value.astype(BF16)
        part = normed.at[position, shard]
        for d in NEAR_FIRST:
            copies.send(("normed", d, position, number), part, part, to_y(d))

    def receive_rows(position):
        for number, d in ((1, 1), (2, 3), (3, 2)):
            copies.wait(("rows", d, position), rows.at[position, at_z(-d)], to_z(d))
            spread_rows(position, number, at_z(-d))

    def receive_normed(position):
        for number, source in enumerate((0, 1, 3, 2)):
            for d in NEAR_FIRST:
                shard = at_y(-d) * 4 + at_z(-source)
                copies.wait(("normed", d, position, number), normed.at[position, shard], to_y(d))

    for position in range(2):
        rows[position, g] = own_rows[position, g]
        spread_rows(position, 0, g)
    quarter_dp("wqkv", qkv_quarter)

    latn[...] = layer_norm(latents_ref[...].astype(F32), latent_gain_ref[...]).astype(BF16)
    queries = dot_nt(query_w_ref[...], latn[...])
    held_queries[...] = jnp.concatenate([queries, queries], axis=1).astype(BF16).reshape(4, 16, 128)
    wkv[q, t, 0:128, :] = jnp.transpose(kv_w_ref[...].astype(F32)).astype(BF16)
    wkv[q, t, 128:144, :] = held_queries[q // 2]

    def unit_start(name, buf, part):
        copies.send((name, "right"), part(buf, q), part(buf, q), to_x(1))
        copies.send((name, "left"), part(buf, q), part(buf, q), to_x(-1))
        copies.send((name, "core", 0), part(buf, q), part(buf, q), sibling)

    def unit_relay(name, buf, part, low, high):
        copies.wait((name, "right"), part(buf, at_x(-1)), to_x(1))
        copies.send((name, "relay_right"), low(buf, at_x(-1)), low(buf, at_x(-1)), to_x(1))
        copies.send((name, "core", 1), part(buf, at_x(-1)), part(buf, at_x(-1)), sibling)
        copies.wait((name, "left"), part(buf, at_x(1)), to_x(-1))
        copies.send((name, "relay_left"), high(buf, at_x(1)), high(buf, at_x(1)), to_x(-1))
        copies.send((name, "core", 2), part(buf, at_x(1)), part(buf, at_x(1)), sibling)

    def unit_far(name, buf, part, low, high):
        copies.wait((name, "relay_right"), low(buf, at_x(2)), to_x(1))
        copies.wait((name, "relay_left"), high(buf, at_x(2)), to_x(-1))
        copies.send((name, "core", 3), part(buf, at_x(2)), part(buf, at_x(2)), sibling)

    def unit_end(name, buf, part):
        for number, d in enumerate((0, -1, 1, 2)):
            other = ((x + d + 4) % 4) * 2 + 1 - c
            copies.wait((name, "core", number), part(buf, other), sibling)

    qkv_unit = (
        "wqkv",
        wqkv,
        lambda buf, at: buf.at[at, pl.ds(1, 3)],
        lambda buf, at: buf.at[at, pl.ds(1, 3), pl.ds(0, 96)],
        lambda buf, at: buf.at[at, pl.ds(1, 3), pl.ds(96, 96)],
    )
    out_unit = (
        "wout",
        wout,
        lambda buf, at: buf.at[at],
        lambda buf, at: buf.at[at, pl.ds(0, 2)],
        lambda buf, at: buf.at[at, pl.ds(2, 2)],
    )

    quarter_dp("wout", out_quarter)
    quarter_end("wqkv", qkv_quarter)
    unit_start(*qkv_unit[:3])
    quarter_end("wout", out_quarter)
    for d in NEAR_FIRST:
        copies.send(f"wout_y{d}", wout.at[q, 0], wout.at[q, d], to_y(d))
    receive_rows(0)
    unit_relay(*qkv_unit)
    for d in NEAR_FIRST:
        copies.send(f"wkv_z{d}", wkv.at[q, t], wkv.at[q, t], to_z(d))
    for d in NEAR_FIRST:
        copies.wait(f"wout_y{d}", wout.at[q, d], to_y(d))
    unit_start(*out_unit[:3])
    receive_rows(1)
    unit_far(*qkv_unit)
    receive_normed(0)
    unit_end(*qkv_unit[:3])
    early = len(copies.started)

    valid = valid_ref[0]
    key_live = lax.broadcasted_iota(jnp.int32, (256, 256), 1) < valid
    first_head = lax.broadcasted_iota(jnp.int32, (256, 128), 1) < 64

    def attend(position):
        here = normed[position].reshape(256, D)
        for pair in range(2):
            blocks = []
            for block in range(8):
                parts = [
                    wqkv[block, 2 * pair + head, kind * 64 : kind * 64 + 64, :]
                    for kind in range(3)
                    for head in range(2)
                ]
                blocks.append(jnp.concatenate(parts, axis=0))
            weight = jnp.concatenate(blocks, axis=1)
            projected = dot_nt(here, weight).astype(BF16)
            query, key, value = (projected[:, k * 128 : k * 128 + 128] for k in range(3))
            mixed = []
            for head in range(2):
                mine = first_head if head == 0 else jnp.logical_not(first_head)
                scores = dot_nt(jnp.where(mine, query, jnp.zeros_like(query)), key) * SCALE
                scores = jnp.where(key_live, scores, -jnp.inf)
                weights = jnp.exp(scores - jnp.max(scores, axis=-1, keepdims=True))
                total = jnp.sum(weights, axis=-1, keepdims=True)
                mixed.append(dot(weights.astype(BF16), value) / total)
            result = jnp.where(first_head, mixed[0], mixed[1]).astype(BF16)
            att_out[position, :, :, pair * 128 : pair * 128 + 128] = result.reshape(4, 64, 128)
        for d in NEAR_FIRST:
            copies.send(
                ("att", d, position), att_out.at[position, at_y(d)], att_in.at[position, d], to_y(d)
            )
        att_in[position, 0] = att_out[position, y]

    def project(position):
        for d in NEAR_FIRST:
            copies.wait(("att", d, position), att_in.at[position, d], to_y(d))
        attended = jnp.concatenate([att_in[position, source] for source in range(4)], axis=1)
        for block in range(4):
            weight = jnp.concatenate(
                [wout[2 * block].reshape(D, 128), wout[2 * block + 1].reshape(D, 128)], axis=1
            )
            cols = slice(block * 256, block * 256 + 256)
            tokens = rows[position, :, :, cols]
            total = tokens.astype(F32).reshape(64, 256) + dot(attended, weight)
            summed[position, :, :, cols] = total.astype(BF16).reshape(4, 16, 256)
        for d in NEAR_FIRST:
            copies.send(
                ("back", d, position), summed.at[position, at_z(d)], back.at[position, g], to_z(d)
            )
        back[position, g] = summed[position, g]

    attend(0)
    unit_relay(*out_unit)
    for d in NEAR_FIRST:
        copies.wait(f"wkv_z{d}", wkv.at[q, y * 4 + at_z(-d)], to_z(d))
    part = wkv.at[q, pl.ds(y * 4, 4)]
    for d in NEAR_FIRST:
        copies.send(("wkv", "y", d), part, part, to_y(d))
    receive_normed(1)
    attend(1)
    unit_far(*out_unit)
    for d in NEAR_FIRST:
        copies.wait(("wkv", "y", d), wkv.at[q, pl.ds(at_y(-d) * 4, 4)], to_y(d))
    for k in NEAR_FIRST:
        there = (x + k) % 4
        part = wkv.at[q, pl.ds(there * 4, 4)]
        copies.send(("wkv", "x", k), part, part, to_x(k))
    own_heads = pl.ds(x * 4, 4)
    copies.send(("wkv", "core", 0), wkv.at[q, own_heads], wkv.at[q, own_heads], sibling)
    unit_end(*out_unit[:3])
    project(0)
    project(1)

    for k in NEAR_FIRST:
        part = wkv.at[at_x(-k), own_heads]
        copies.wait(("wkv", "x", k), part, to_x(k))
        copies.send(("wkv", "core", k), part, part, sibling)
    copies.drain(early)
    copies.wait("start_after", start_in.at[0], after)
    copies.wait("start_before", start_in.at[1], before)

    pool_gain = pool_gain_ref[...]

    def pool_norm(position, number, source):
        value = layer_norm(back[position, source].astype(F32), pool_gain)
        pooled[x, position, source] = value.astype(BF16)
        part = pooled.at[x, position, source]
        for k in NEAR_FIRST:
            copies.send(("pooled", k, position, number), part, part, to_x(k))

    def receive_back(position):
        for number, d in ((1, 1), (2, 3), (3, 2)):
            copies.wait(("back", d, position), back.at[position, at_z(-d)], to_z(d))
            pool_norm(position, number, at_z(-d))

    pool_norm(0, 0, g)
    pool_norm(1, 0, g)
    for d in (0,) + NEAR_FIRST:
        other = ((x - d + 4) % 4) * 2 + 1 - c
        copies.wait(("wkv", "core", d), wkv.at[other, own_heads], sibling)

    wide_lane = lax.broadcasted_iota(jnp.int32, (64, 256), 1)
    for head in range(4):
        parts = [wkv[2 * block, 4 * x + head, 128:144, :] for block in range(4)]
        query = jnp.concatenate(parts, axis=0)
        query = jnp.concatenate([query, query], axis=1)
        block_queries[head * 64 : head * 64 + 64, :] = jnp.where(
            (wide_lane >> 6) == head, query, jnp.zeros_like(query)
        )

    key_blocks, value_blocks = [], []
    for block in range(8):
        two = wkv[block, pl.ds(q * 2, 2)]
        key_blocks.append(two[:, 0:64, :].reshape(128, 128))
        value_blocks.append(two[:, 64:128, :].reshape(128, 128))
    self_key = dot_nt(latn[...], jnp.concatenate(key_blocks, axis=1)).astype(BF16)
    self_value = dot_nt(jnp.concatenate(value_blocks, axis=1), latn[...]).astype(BF16)
    pair_queries = jnp.where(
        c == 0, block_queries[0:128, 0:128], block_queries[128:256, 128:256]
    )
    self_scores = dot(self_key, pair_queries) * SCALE
    self_top = jnp.max(self_scores, axis=0, keepdims=True)

    for position in range(2):
        receive_back(position)

    far_starts = jnp.where(lane < 64, start_in[1], start_in[0])[0:1]
    own_starts = start_out[0:1, :]
    frame = t * 16 + (lax.broadcasted_iota(jnp.int32, (128, 256), 0) & 15)
    in_lane = lax.broadcasted_iota(jnp.int32, (1, 128), 1)

    def live_of(starts, second):
        half = jnp.where((in_lane >= 64) == second, starts, -(10**6))
        start = jnp.max(half, axis=1, keepdims=True)
        return (frame >= start) & (frame < start + CLIP) & (frame < valid)

    live = [
        live_of(own_starts, False),
        live_of(own_starts, True),
        live_of(far_starts, False),
        live_of(far_starts, True),
    ]
    pair_lane = lax.broadcasted_iota(jnp.int32, (64, 128), 1)
    key_blocks, value_blocks = [], []
    for block in range(8):
        four = wkv[block, own_heads]
        key_blocks.append(four[:, 0:64, :].reshape(256, 128))
        value_blocks.append(four[:, 64:128, :].reshape(256, 128))
    key_weight = jnp.concatenate(key_blocks, axis=1)
    value_weight = jnp.concatenate(value_blocks, axis=1)

    def pool_project(place, source):
        here = pooled[source].reshape(128, D)
        key = dot_nt(here, key_weight).astype(BF16)
        scores_at[place] = dot(key, block_queries[...]) * SCALE
        values[:, place * 128 : place * 128 + 128] = dot_nt(value_weight, here).astype(BF16)

    pool_project(0, x)

    by_frame = jnp.where(
        from_row == (to_row & 1) * 64 + ((to_row & 7) >> 1) * 16 + (to_row >> 3), 1.0, 0.0
    ).astype(BF16)
    held = back[...].reshape(128, D)
    for half in range(2):
        cols = slice(half * 512, half * 512 + 512)
        temporal_ref[:, cols] = dot(by_frame, held[:, cols]).astype(BF16)
    for place, k in ((1, 1), (2, 3), (3, 2)):
        source = (x - k + 4) % 4
        for position in range(2):
            for number, d in enumerate((0, 1, 3, 2)):
                part = pooled.at[source, position, at_z(-d)]
                copies.wait(("pooled", k, position, number), part, to_x(k))
        pool_project(place, source)

    for clip in range(4):
        top = jnp.full((1, 256), NEG, F32)
        for place in range(4):
            kept = jnp.where(live[clip], scores_at[place], NEG)
            top = jnp.maximum(top, jnp.max(kept, axis=0, keepdims=True))
        weights = [
            jnp.where(live[clip], jnp.exp(scores_at[place] - top), 0.0) for place in range(4)
        ]
        total = sum(jnp.sum(weight, axis=0, keepdims=True) for weight in weights)
        mix = dot(values[...], jnp.concatenate([w.astype(BF16) for w in weights], axis=0))
        for pair in range(2):
            cols = slice(pair * 128, pair * 128 + 128)
            even = mix[pair * 128 : pair * 128 + 64, cols]
            odd = mix[pair * 128 + 64 : pair * 128 + 128, cols]
            part_out[pair, clip * 64 : clip * 64 + 64, :] = jnp.where(
                pair_lane < 64, even, odd
            ).astype(BF16)
            stat_out[pair, clip : clip + 1, :] = top[:, cols]
            stat_out[pair, 4 + clip : 5 + clip, :] = total[:, cols]
    copies.send("part", part_out.at[1 - c], part_in, sibling)
    copies.send("stat", stat_out.at[1 - c], stat_in, sibling)

    copies.wait("part", part_in, sibling)
    copies.wait("stat", stat_in, sibling)
    stats = [stat_out[c], stat_in[...]]
    highest = stats[0][0:4]
    for stat in stats[1:]:
        highest = jnp.maximum(highest, stat[0:4])
    factors = [jnp.exp(stat[0:4] - highest) for stat in stats]
    totals = jnp.zeros((4, 128), F32)
    for stat, factor in zip(stats, factors):
        totals += stat[4:8] * factor
    nstat_out[0:4, :] = highest
    nstat_out[4:8, :] = totals

    def gathered(clip):
        mix = jnp.zeros((64, 128), F32)
        span = slice(clip * 64, clip * 64 + 64)
        for part, factor in zip((part_out[c, span, :], part_in[span, :]), factors):
            mix += part.astype(F32) * factor[clip : clip + 1]
        return mix

    near_out[0] = gathered(2).astype(BF16)
    copies.send("near_after", near_out.at[0], near_in.at[0], after)
    copies.send("nstat_after", nstat_out, nstat_in.at[0], after)
    near_out[1] = gathered(3).astype(BF16)
    copies.send("near_before", near_out.at[1], near_in.at[1], before)
    copies.send("nstat_before", nstat_out, nstat_in.at[1], before)
    own_mixes = [gathered(0), gathered(1)]

    finished = []
    for clip, name, device in ((0, "after", after), (1, "before", before)):
        copies.wait(f"near_{name}", near_in.at[clip], device)
        copies.wait(f"nstat_{name}", nstat_in.at[clip], device)
        near_top = nstat_in[clip, 2 + clip : 3 + clip, :]
        near_total = nstat_in[clip, 6 + clip : 7 + clip, :]
        own_top = highest[clip : clip + 1]
        top = jnp.maximum(jnp.maximum(own_top, near_top), self_top)
        own_factor = jnp.exp(own_top - top)
        near_factor = jnp.exp(near_top - top)
        weights = jnp.exp(self_scores - top)
        total = (
            totals[clip : clip + 1] * own_factor
            + near_total * near_factor
            + jnp.sum(weights, axis=0, keepdims=True)
        )
        self_mix = dot(self_value, weights.astype(BF16))
        self_mix = jnp.where(pair_lane < 64, self_mix[0:64], self_mix[64:128])
        mix = own_mixes[clip] * own_factor + near_in[clip].astype(F32) * near_factor + self_mix
        finished.append(mix / total)

    turned = jnp.transpose(jnp.concatenate(finished, axis=0))
    even, odd = turned[0:64], turned[64:128]
    piece_out[0:64, :] = jnp.where(pair_lane < 64, even, pltpu.roll(odd, 64, 1)).astype(BF16)
    piece_out[64:128, :] = jnp.where(pair_lane < 64, pltpu.roll(even, 64, 1), odd).astype(BF16)
    for d in range(1, 8):
        copies.send(("piece", d), piece_out, piece_in.at[q], to_patch(d))
    piece_in[q] = piece_out[...]
    for d in range(1, 8):
        copies.wait(("piece", d), piece_in.at[(q + 8 - d) % 8], to_patch(d))
    for block in range(8):
        pooled_ref[:, block * 128 : block * 128 + 128] = piece_in[block]
    copies.drain()
    assert len(copies.slots) <= SLOTS


def on_device(
    tokens,
    frame_gain,
    qkv_weight,
    out_weight,
    pool_gain,
    latent_gain,
    latents,
    query_weight,
    kv_weight,
    clip_starts,
    valid_frames,
):
    frames_dev, patch_dev, width = tokens.shape
    vmem = pl.BlockSpec(memory_space=pltpu.VMEM)
    temporal_out, pooled = pl.pallas_call(
        kernel,
        out_shape=(
            jax.ShapeDtypeStruct((128, D), BF16),
            jax.ShapeDtypeStruct((128, D), BF16),
        ),
        in_specs=[pl.BlockSpec(memory_space=pl.ANY)] * 11,
        out_specs=(vmem, vmem),
        scratch_shapes=[
            pltpu.SMEM((2,), jnp.int32),
            pltpu.SMEM((1,), jnp.int32),
            pltpu.VMEM((128, D), BF16),
            pltpu.VMEM((1, D), F32),
            pltpu.VMEM((1, D), F32),
            pltpu.VMEM((1, D), F32),
            pltpu.VMEM((64, D), BF16),
            pltpu.VMEM((64, D), BF16),
            pltpu.VMEM((128, 128), BF16),
            pltpu.VMEM((2, 4, 16, D), BF16),
            pltpu.VMEM((2, 4, 16, D), BF16),
            pltpu.VMEM((2, 16, 16, D), BF16),
            pltpu.VMEM((8, 4, 192, 128), BF16),
            pltpu.VMEM((8, 4, 4, 64, 128), BF16),
            pltpu.VMEM((8, 16, 144, 128), BF16),
            pltpu.VMEM((2, 4, 64, 256), BF16),
            pltpu.VMEM((2, 4, 64, 256), BF16),
            pltpu.VMEM((2, 4, 16, D), BF16),
            pltpu.VMEM((2, 4, 16, D), BF16),
            pltpu.VMEM((4, 2, 4, 16, D), BF16),
            pltpu.VMEM((64, D), BF16),
            pltpu.VMEM((4, 16, 128), BF16),
            pltpu.VMEM((256, 256), BF16),
            pltpu.VMEM((4, 128, 256), F32),
            pltpu.VMEM((256, 512), BF16),
            pltpu.VMEM((8, 128), jnp.int32),
            pltpu.VMEM((2, 8, 128), jnp.int32),
            pltpu.VMEM((2, 256, 128), BF16),
            pltpu.VMEM((256, 128), BF16),
            pltpu.VMEM((2, 8, 128), F32),
            pltpu.VMEM((8, 128), F32),
            pltpu.VMEM((2, 64, 128), BF16),
            pltpu.VMEM((2, 64, 128), BF16),
            pltpu.VMEM((8, 128), F32),
            pltpu.VMEM((2, 8, 128), F32),
            pltpu.VMEM((128, 128), BF16),
            pltpu.VMEM((8, 128, 128), BF16),
            pltpu.SemaphoreType.DMA((18,)),
            pltpu.SemaphoreType.DMA((SLOTS,)),
            pltpu.SemaphoreType.DMA((SLOTS,)),
        ],
        compiler_params=pltpu.CompilerParams(
            collective_id=0, has_side_effects=True, vmem_limit_bytes=62 * 1024 * 1024
        ),
    )(
        clip_starts,
        valid_frames,
        tokens.reshape(frames_dev * patch_dev, width),
        frame_gain.reshape(1, width),
        qkv_weight.T,
        out_weight,
        pool_gain.reshape(1, width),
        latent_gain.reshape(1, width),
        latents,
        query_weight.T,
        kv_weight,
    )
    return (
        temporal_out.reshape(frames_dev, patch_dev, width),
        pooled.reshape(2, 64, width),
    )


def solution(mesh):
    in_specs = (
        P(("dp", "tm"), "patch", None),
        P(),
        P(None, "tm"),
        P("tm", None),
        P(),
        P(),
        P(),
        P(None, "tm"),
        P(None, "tm"),
        P(("dp", "tm")),
        P("dp"),
    )
    out_specs = (P(("dp", "tm"), "patch", None), P(("dp", "tm"), None, None))
    return jax.shard_map(
        on_device, mesh=mesh, in_specs=in_specs, out_specs=out_specs, check_vma=False
    )
```
